32 devices in a mesh: pos: 8 (over y, x, core), vel: 4 (over z).
Axes of the slice: x: 2, y: 2, z: 4, core: 2. Of those that a mesh axis runs over, the one named last changes fastest.
Arguments:
- density: float32 [4, 512, 512], P(None, 'pos', 'vel'), may hold values from 0.25 to 4
- pos_coef: float32 [512, 512], P('pos', 'vel'), may hold values from 2000 to 16000
- vel_coef: float32 [512, 512], P('pos', 'vel'), may hold values from 4000 to 32000
- exit_mask: int32 [512, 512], P('pos', 'vel'), may hold values from 0 to 1, as said below
- phase_index: int32 [4], replicated, may hold values from 0 to 63
Outputs:
- new_density: float32 [4, 512, 512], P(None, 'pos', 'vel')
- absorbed: float32 [512, 512], P('pos', 'vel')
The draws below stay inside these ranges and needn't reach their ends.
Inputs may be any that keep to these rules, and one draw needn't show every extreme that they name: exit_mask is 1 on every cell whose xpos lies beyond 1.3 in magnitude, and on scattered cells elsewhere.
All inputs are finite; a program needn't handle non-finite values.
Results may differ from the reference program's by a relative error of at most 0.0003.
Values sent between devices are 32-bit elements; how exact they have to be, the bound alone decides.
A program may use at most 64 MiB of HBM per device.

```python
import math
import jax
import jax.numpy as jnp
from jax import lax

P_SIZE = 4
STEPS = 2
NPHASE = 64
NX = 512
NV = 512


def draw_exit_mask(key, part):
    rows = jnp.arange(NX, dtype=jnp.int32)[:, None]
    twice = 2 * rows + 1
    band = (15 * twice > 28 * NX) | (15 * twice < 2 * NX)
    scattered = jax.random.randint(key, (NX, NV), 0, 32) == 0
    return (band | scattered).astype(jnp.int32)


def place_ends(entries, stream_key, low, largest):
    index_at = [jax.random.randint(jax.random.fold_in(stream_key, axis), (), 0, length) for axis, length in enumerate(entries.shape)]
    main_axis = entries.shape.index(max(entries.shape))
    beside = index_at[:main_axis] + [(index_at[main_axis] + 1) % entries.shape[main_axis]] + index_at[main_axis + 1:]
    return entries.at[tuple(index_at)].set(low).at[tuple(beside)].set(largest)


def block_scale(rng, dims, cuts, low, top_value):
    def one(axis_at, parts):
        draws = jax.random.uniform(jax.random.fold_in(jax.random.fold_in(rng, 6), axis_at), (parts,), jnp.float32, low / len(cuts), top_value / len(cuts))
        return jnp.repeat(jnp.exp(draws), dims[axis_at] // parts).reshape((-1,) + (1,) * (len(dims) - axis_at - 1))

    factor_of = one(*cuts[0])
    for cut in cuts[1:]:
        factor_of = factor_of * one(*cut)
    return factor_of


def setup_inputs(seed: int = 0) -> dict:
    arg_keys = jax.random.split(jax.random.key(seed), 6)
    density = jnp.clip(jnp.exp(math.log(4.0) - 2.7725887 * jax.random.uniform(arg_keys[0], (P_SIZE, NX, NV), jnp.float32) ** block_scale(arg_keys[0], (P_SIZE, NX, NV), ((1, 8), (2, 4)), -0.2, 0.2)), 0.25, 4.0)
    pos_coef = jnp.clip(jnp.exp(math.log(16000.0) - 2.0794415 * jax.random.uniform(arg_keys[1], (NX, NV), jnp.float32) ** block_scale(arg_keys[1], (NX, NV), ((0, 8), (1, 4)), -0.2, 0.2)), 2000.0, 16000.0)
    vel_coef = jnp.clip(jnp.exp(math.log(32000.0) - 2.0794415 * jax.random.uniform(arg_keys[2], (NX, NV), jnp.float32) ** block_scale(arg_keys[2], (NX, NV), ((0, 8), (1, 4)), -0.2, 0.2)), 4000.0, 32000.0)
    exit_mask = draw_exit_mask(jax.random.fold_in(arg_keys[5], 71), 0)
    phase_index = place_ends(jax.random.randint(arg_keys[4], (P_SIZE,), 0, NPHASE), jax.random.fold_in(arg_keys[4], 1), 0, NPHASE - 1).astype(jnp.int32)
    return dict(density=density, pos_coef=pos_coef, vel_coef=vel_coef, exit_mask=exit_mask, phase_index=phase_index)


def thomas(below, middle, above, source):
    zero = jnp.zeros_like(source[0])

    def downward(carry, row):
        prior_up, prior_src = carry
        row_low, row_mid, row_up, row_src = row
        factor = 1.0 / (row_mid - row_low * prior_up)
        result = (factor * row_up, factor * (row_src - row_low * prior_src))
        return result, result

    _, (sweep_up, sweep_src) = lax.scan(downward, (zero, zero), (below, middle, above, source))

    def upward(later, row):
        row_up, row_src = row
        value = row_src - row_up * later
        return value, value

    _, solved = lax.scan(upward, zero, (sweep_up, sweep_src), reverse=True)
    return solved


def drift(padded, move_rate, force_rate):
    center = padded[:, 1:-1, 1:-1]
    back_x = padded[:, :-2, 1:-1]
    ahead_x = padded[:, 2:, 1:-1]
    back_v = padded[:, 1:-1, :-2]
    ahead_v = padded[:, 1:-1, 2:]
    along_x = jnp.maximum(move_rate, 0.0) * (center - back_x) + jnp.minimum(move_rate, 0.0) * (ahead_x - center)
    along_v = jnp.maximum(force_rate, 0.0) * (center - back_v) + jnp.minimum(force_rate, 0.0) * (ahead_v - center)
    return center - along_x - along_v


def bands(coef, length):
    rows = jnp.arange(length)[:, None]
    below = jnp.where(rows == 0, 0.0, -coef)
    above = jnp.where(rows == length - 1, 0.0, -coef)
    middle = 1.0 + 2.0 * coef
    return below[:, None, :], middle[:, None, :], above[:, None, :]


def reference(density, pos_coef, vel_coef, exit_mask, phase_index):
    xpos = 1.5 * ((2.0 * jnp.arange(NX).astype(jnp.float32) + 1.0) / NX - 1.0)
    vpos = (2.0 * jnp.arange(NV).astype(jnp.float32) + 1.0) / NV - 1.0
    theta = 2.0 * math.pi * phase_index.astype(jnp.float32) / NPHASE
    force = (xpos - xpos * xpos * xpos)[None, :, None] + 0.6 * jnp.cos(theta)[:, None, None] - 0.5 * vpos[None, None, :]
    move_rate = 0.45 * vpos[None, None, :]
    force_rate = 0.15 * force
    hit = exit_mask.astype(jnp.float32)
    keep = 1.0 - hit
    below_x, middle_x, above_x = bands(pos_coef, NX)
    below_v, middle_v, above_v = bands(vel_coef.T, NV)
    field = density
    absorbed = jnp.zeros((NX, NV), jnp.float32)
    for step in range(STEPS):
        padded = jnp.pad(field, ((0, 0), (1, 1), (1, 1)))
        drifted = drift(padded, move_rate, force_rate)
        absorbed = absorbed + jnp.sum(drifted, axis=0) * hit
        kept = drifted * keep[None]
        swept = jnp.moveaxis(thomas(below_x, middle_x, above_x, jnp.moveaxis(kept, 1, 0)), 0, 1)
        solved = jnp.moveaxis(thomas(below_v, middle_v, above_v, jnp.moveaxis(swept, 2, 0)), 0, 2)
        field = solved * keep[None]
    return field, absorbed
```

```python
import functools
import math

import jax
import jax.numpy as jnp
from jax import lax
from jax.experimental import pallas as pl
from jax.experimental.pallas import tpu as pltpu
from jax.sharding import PartitionSpec as P

STEPS = 2
NPHASE = 64
SUB = 8
MESH = pl.DeviceIdType.MESH


def coef_chain(low, high, excess):
    inv, carry_low, ups, lows, rest = [], [], [], [], []
    for t in range(len(low)):
        if t == 0:
            left_low, left_rest = low[0], excess[0]
        else:
            left_low, left_rest = low[t] * lows[-1], low[t] * rest[-1] + excess[t]
        factor = 1.0 / (left_low + left_rest + high[t])
        inv.append(factor)
        carry_low.append(low[t] * factor)
        ups.append(high[t] * factor)
        lows.append(left_low * factor)
        rest.append(left_rest * factor)
    beta, gamma, eps = lows[-1], ups[-1], rest[-1]
    betas, gammas, epss = [beta], [gamma], [eps]
    for t in range(len(low) - 2, -1, -1):
        beta = lows[t] + ups[t] * beta
        gamma = ups[t] * gamma
        eps = rest[t] + ups[t] * eps
        betas.append(beta)
        gammas.append(gamma)
        epss.append(eps)
    return inv, carry_low, ups, betas[::-1], gammas[::-1], epss[::-1]


def source_chain(chain, source):
    inv, carry_low, ups = chain[:3]
    forward = [source[0] * inv[0]]
    for t in range(1, len(source)):
        forward.append(source[t] * inv[t] + carry_low[t] * forward[-1])
    own = [forward[-1]]
    for t in range(len(source) - 2, -1, -1):
        own.append(forward[t] + ups[t] * own[-1])
    return own[::-1]


def next_sub(x, axis):
    return pltpu.roll(x, SUB - 1, axis)


def factor_block(coef, store_row):
    one = jnp.ones_like(coef[0])
    inner = coef_chain(coef[:-1], coef[:-1], [one] * (len(coef) - 1))
    beta, gamma, eps = inner[3:]
    last = coef[-1]
    low = last * beta[-1]
    high = last * next_sub(gamma[0], 0)
    excess = 1.0 + last * eps[-1] + last * next_sub(eps[0], 0)
    rows = lambda x: [x[s : s + 1] for s in range(SUB - 1)]
    outer = coef_chain(rows(low), rows(high), rows(excess))
    obeta, ogamma, oeps = outer[3:]
    end = slice(SUB - 1, SUB)
    first_gamma = gamma[0][0:1]
    store_row(0, beta[0][0:1] + first_gamma * obeta[0])
    store_row(1, first_gamma * ogamma[0])
    store_row(2, eps[0][0:1] + first_gamma * oeps[0])
    store_row(3, last[end])
    store_row(4, low[end] * obeta[-1])
    store_row(5, 1.0 + last[end] * eps[-1][end] + low[end] * oeps[-1])
    return inner, outer, last, first_gamma, low[end]


def eliminate(block, source, hold_a, hold_b):
    inner, outer, last, first_gamma, end_low = block
    planes = source[0].shape[0]
    own = source_chain(inner, source[:-1])
    sub = lax.broadcasted_iota(jnp.int32, source[0].shape, 1)
    after = jnp.where(sub == SUB - 1, 0.0, next_sub(own[0], 1))
    seps = source[-1] + last * (own[-1] + after)
    hold_a[...] = seps.reshape(hold_a.shape)
    hold_b[...] = own[0].reshape(hold_b.shape)
    row = lambda ref, s: ref[pl.ds(s, planes, stride=SUB), :]
    outer_own = source_chain(outer, [row(hold_a, s) for s in range(SUB - 1)])
    first = row(hold_b, 0) + first_gamma * outer_own[0]
    own_end = row(hold_a, SUB - 1) + end_low * outer_own[-1]
    return own, outer_own, first, own_end


def finish(block, own, outer_own, before, end, hold_a, hold_b):
    inner, outer = block[:2]
    planes = before.shape[0]
    hold_b[pl.ds(0, planes, stride=SUB), :] = before
    for s in range(SUB - 1):
        value = outer_own[s] + outer[3][s] * before + outer[4][s] * end
        hold_a[pl.ds(s, planes, stride=SUB), :] = value
        hold_b[pl.ds(s + 1, planes, stride=SUB), :] = value
    hold_a[pl.ds(SUB - 1, planes, stride=SUB), :] = end
    right = hold_a[...].reshape(own[0].shape)
    left = hold_b[...].reshape(own[0].shape)
    return [p + b * left + g * right for p, b, g in zip(own, inner[3], inner[4])] + [right]


def reduced_coefs(buf, count):
    kept, rest = [], 1.0
    for d in range(count):
        link = buf[d, 3:4, :]
        left = buf[d, 4:5, :]
        high = link * buf[d + 1, 1:2, :]
        excess = left * rest + buf[d, 5:6, :] + link * buf[d + 1, 2:3, :]
        factor = 1.0 / (excess + high)
        rest = excess * factor
        kept.append((factor, left * factor, high * factor, link * factor))
    return kept


def reduced_solve(kept, buf, step, whole, count, planes):
    forward, prior = [], None
    for d in range(count):
        factor, left, _, link = kept[d]
        value = factor * buf[step, d, planes : 2 * planes, :] + link * buf[step, d + 1, 0:planes, :]
        prior = value if prior is None else value + left * prior
        forward.append(prior)
    value = forward[-1]
    whole[count] = value
    for d in range(count - 2, -1, -1):
        value = forward[d] + kept[d][2] * value
        whole[d + 1] = value


def kernel(
    npos, nvel, planes, cells, width,
    dens, pcoef, vcoef, mask, phase,
    out, taken,
    ext, turned, edge_tmp, vext, pos_edge, vel_edge, pos_edge_in, vel_edge_in,
    pos_cbuf, vel_cbuf, pos_buf, vel_buf, pos_whole, vel_whole, hold_a, hold_b,
    edge_send, edge_recv, psend, precv, vsend, vrecv,
):
    lanes = width
    mp, mv = cells // SUB, width // SUB
    ipos, ivel = lax.axis_index("pos"), lax.axis_index("vel")

    pos_id = lambda d: (d, ivel)
    vel_id = lambda d: (ipos, d)

    barrier = pltpu.get_barrier_semaphore()

    def greet(count, me, ident):
        for off in range(1, count):
            peer = lax.rem(me + off, count)
            pl.semaphore_signal(barrier, 1, device_id=ident(peer), device_id_type=MESH)

    pos_edge_in[...] = jnp.zeros_like(pos_edge_in)
    vel_edge_in[...] = jnp.zeros_like(vel_edge_in)
    greet(npos, ipos, pos_id)
    greet(nvel, ivel, vel_id)
    ext[...] = jnp.zeros_like(ext)
    vext[...] = jnp.zeros_like(vext)
    edge_tmp[...] = jnp.zeros_like(edge_tmp)
    for cbuf, buf, whole, count in (
        (pos_cbuf, pos_buf, pos_whole, npos),
        (vel_cbuf, vel_buf, vel_whole, nvel),
    ):
        sub = lax.broadcasted_iota(jnp.int32, (8, lanes), 0)
        cbuf[count] = jnp.where(sub == 2, 1.0, 0.0)
        buf[0, count] = jnp.zeros((2 * planes, lanes), jnp.float32)
        buf[1, count] = jnp.zeros((2 * planes, lanes), jnp.float32)
        whole[0] = jnp.zeros((planes, lanes), jnp.float32)
        whole[count + 1] = jnp.zeros((planes, lanes), jnp.float32)

    hit = mask[...].astype(jnp.float32)
    pos_edge[...] = jnp.zeros_like(pos_edge)
    for p in range(planes):
        pos_edge[p : p + 1, :] = dens[p * cells : p * cells + 1, :]
        pos_edge[planes + p : planes + p + 1, :] = dens[(p + 1) * cells - 1 : (p + 1) * cells, :]
    pos_edge[2 * planes : 2 * planes + 1, :] = hit[0:1]
    pos_edge[2 * planes + 1 : 2 * planes + 2, :] = hit[cells - 1 : cells]
    pos_edge[2 * planes + 2 : 2 * planes + 3, :] = vcoef[0:1, :]
    pos_edge[2 * planes + 3 : 2 * planes + 4, :] = vcoef[cells - 1 : cells, :]
    lane = lax.broadcasted_iota(jnp.int32, (cells, lanes), 1)
    gathered = jnp.zeros((cells, lanes), jnp.float32)
    for p in range(planes):
        one = dens[p * cells : (p + 1) * cells, :]
        gathered = jnp.where(lane == p, one[:, 0:1], gathered)
        gathered = jnp.where(lane == planes + p, one[:, lanes - 1 : lanes], gathered)
    gathered = jnp.where(lane == 2 * planes, hit[:, 0:1], gathered)
    gathered = jnp.where(lane == 2 * planes + 1, hit[:, lanes - 1 : lanes], gathered)
    edge_tmp[0:cells, :] = gathered
    vel_edge[...] = edge_tmp[...].T[0:16]

    pl.semaphore_wait(barrier, (npos - 1) + (nvel - 1))

    def edge_copy(axis, to_right, src, dst, ident, me):
        slot = 0 if to_right else 1
        peer = me + 1 if to_right else me - 1
        return pltpu.make_async_remote_copy(
            src_ref=src, dst_ref=dst.at[slot],
            send_sem=edge_send.at[axis, slot], recv_sem=edge_recv.at[axis, slot],
            device_id=ident(peer), device_id_type=MESH,
        )

    sides = (
        (0, pos_edge, pos_edge_in, pos_id, ipos, npos),
        (1, vel_edge, vel_edge_in, vel_id, ivel, nvel),
    )

    def edge_each(which, act):
        axis, src, dst, ident, me, count = sides[which]

        @pl.when(me < count - 1)
        def _():
            act(edge_copy(axis, True, src, dst, ident, me), True)

        @pl.when(me > 0)
        def _():
            act(edge_copy(axis, False, src, dst, ident, me), False)

    def edge_wait(which):
        axis, src, dst, ident, me, count = sides[which]

        @pl.when(me > 0)
        def _():
            edge_copy(axis, True, src, dst, ident, me).wait_recv()

        @pl.when(me < count - 1)
        def _():
            edge_copy(axis, False, src, dst, ident, me).wait_recv()

    edge_each(0, lambda c, _: c.start())
    edge_each(1, lambda c, _: c.start())

    def spread_copy(ref, kind, sends, recvs, ident, me, count, off):
        peer = lax.rem(me + off, count)
        return pltpu.make_async_remote_copy(
            src_ref=ref.at[me], dst_ref=ref.at[me],
            send_sem=sends.at[kind, off], recv_sem=recvs.at[kind, me],
            device_id=ident(peer), device_id_type=MESH,
        )

    def spread(*args):
        for off in range(1, args[-1]):
            spread_copy(*args, off).start()

    def spread_wait_recv(ref, kind, sends, recvs, ident, me, count):
        for off in range(1, count):
            sender = lax.rem(me + off, count)
            pltpu.make_async_remote_copy(
                src_ref=ref.at[sender], dst_ref=ref.at[sender],
                send_sem=sends.at[kind, off], recv_sem=recvs.at[kind, sender],
                device_id=ident(sender), device_id_type=MESH,
            ).wait_recv()

    def spread_wait_send(*args):
        for off in range(1, args[-1]):
            spread_copy(*args, off).wait_send()

    pos_coef_args = (pos_cbuf, 0, psend, precv, pos_id, ipos, npos)
    vel_coef_args = (vel_cbuf, 0, vsend, vrecv, vel_id, ivel, nvel)
    pos_args = [(pos_buf.at[i], 1 + i, psend, precv, pos_id, ipos, npos) for i in range(STEPS)]
    vel_args = [(vel_buf.at[i], 1 + i, vsend, vrecv, vel_id, ivel, nvel) for i in range(STEPS)]

    pos_cbuf[ipos] = jnp.zeros((8, lanes), jnp.float32)

    def pos_row(r, value):
        pos_cbuf[ipos, r : r + 1, :] = value

    pos_block = factor_block([pcoef[pl.ds(t, SUB, stride=mp), :] for t in range(mp)], pos_row)
    spread(*pos_coef_args)

    sub = lax.broadcasted_iota(jnp.int32, (SUB, lanes), 0)
    lane = lax.broadcasted_iota(jnp.int32, (SUB, lanes), 1)
    turns = jnp.zeros((SUB, lanes), jnp.int32)
    for p in range(planes):
        turns = jnp.where(sub == p, phase[p], turns)
    cosine = 0.6 * jnp.cos(2.0 * math.pi * turns.astype(jnp.float32) / NPHASE)
    vpos = (2.0 * (ivel * width + lane).astype(jnp.float32) + 1.0) * (1.0 / (width * nvel)) - 1.0
    move = 0.45 * vpos
    move_up, move_down = jnp.maximum(move, 0.0), jnp.minimum(move, 0.0)
    cosines = jnp.stack([jnp.broadcast_to(cosine[p : p + 1], (SUB, lanes)) for p in range(planes)])

    def drift(step, field, row_before, row_after, columns):
        edge_tmp[0 : 2 * planes, :] = columns
        if step > 0:
            edge_tmp[2 * planes : 16, :] = jnp.zeros((16 - 2 * planes, lanes), jnp.float32)
        turned[0:lanes, :] = edge_tmp[...].T
        wide_sub = lax.broadcasted_iota(jnp.int32, (planes, SUB, lanes), 1)
        wide_lane = lax.broadcasted_iota(jnp.int32, (planes, SUB, lanes), 2)
        before = jnp.where(wide_sub == 0, row_before[:, None, :], pltpu.roll(field[-1], 1, 1))
        after = jnp.where(wide_sub == SUB - 1, row_after[:, None, :], next_sub(field[0], 1))
        kept = []
        for t in range(mp):
            xpos = 1.5 * (
                (2.0 * (ipos * cells + sub * mp + t).astype(jnp.float32) + 1.0)
                * (1.0 / (cells * npos))
                - 1.0
            )
            rate = 0.15 * (((xpos - xpos * xpos * xpos)[None] + cosines) - (0.5 * vpos)[None])
            center = field[t]
            back = field[t - 1] if t else before
            ahead = field[t + 1] if t < mp - 1 else after
            cols = turned[pl.ds(t, SUB, stride=mp), :]
            left = jnp.stack([cols[:, p : p + 1] for p in range(planes)])
            right = jnp.stack([cols[:, planes + p : planes + p + 1] for p in range(planes)])
            back_v = jnp.where(wide_lane == 0, left, pltpu.roll(center, 1, 2))
            ahead_v = jnp.where(wide_lane == lanes - 1, right, pltpu.roll(center, lanes - 1, 2))
            along_x = move_up * (center - back) + move_down * (ahead - center)
            along_v = jnp.maximum(rate, 0.0) * (center - back_v) + jnp.minimum(rate, 0.0) * (
                ahead_v - center
            )
            drifted = center - along_x - along_v
            hit_t = mask[pl.ds(t, SUB, stride=mp), :].astype(jnp.float32)
            took = jnp.sum(drifted, axis=0) * hit_t
            if step > 0:
                took = taken[pl.ds(t, SUB, stride=mp), :] + took
            taken[pl.ds(t, SUB, stride=mp), :] = took
            kept.append(drifted * (1.0 - hit_t))
        return kept

    edge_wait(1)
    edge_wait(0)
    row_before = pos_edge_in[0, planes : 2 * planes, :]
    row_after = pos_edge_in[1, 0:planes, :]
    keep_before = 1.0 - pos_edge_in[0, 2 * planes + 1 : 2 * planes + 2, :]
    keep_after = 1.0 - pos_edge_in[1, 2 * planes : 2 * planes + 1, :]
    col_keep_left = 1.0 - vel_edge_in[0, 2 * planes + 1 : 2 * planes + 2, :]
    col_keep_right = 1.0 - vel_edge_in[1, 2 * planes : 2 * planes + 1, :]
    columns = jnp.concatenate(
        [vel_edge_in[0, planes : 2 * planes, :], vel_edge_in[1, 0:planes, :]], axis=0
    )
    field = [
        jnp.stack([dens[pl.ds(p * cells + t, SUB, stride=mp), :] for p in range(planes)])
        for t in range(mp)
    ]
    vel_block = pos_kept = vel_kept = None

    for step in range(STEPS):
        kept = drift(step, field, row_before, row_after, columns)
        own, outer_own, first, own_end = eliminate(pos_block, kept, hold_a, hold_b)
        pos_buf[step, ipos, 0:planes, :] = first
        pos_buf[step, ipos, planes : 2 * planes, :] = own_end
        spread(*pos_args[step])
        if step == 0:
            vext[0:cells, :] = vcoef[...]
            vext[cells : cells + 1, :] = pos_edge_in[0, 2 * planes + 3 : 2 * planes + 4, :]
            vext[cells + 1 : cells + 2, :] = pos_edge_in[1, 2 * planes + 2 : 2 * planes + 3, :]
            turned[0:width, :] = vext[...].T
            vel_cbuf[ivel] = jnp.zeros((8, lanes), jnp.float32)

            def vel_row(r, value):
                vel_cbuf[ivel, r : r + 1, :] = value

            vel_block = factor_block(
                [turned[pl.ds(t, SUB, stride=mv), :] for t in range(mv)], vel_row
            )
            spread(*vel_coef_args)
            spread_wait_recv(*pos_coef_args)
            pos_kept = reduced_coefs(pos_cbuf, npos)
        spread_wait_recv(*pos_args[step])
        reduced_solve(pos_kept, pos_buf, step, pos_whole, npos, planes)
        before, end, beyond = pos_whole[ipos], pos_whole[ipos + 1], pos_whole[ipos + 2]
        swept = finish(pos_block, own, outer_own, before, end, hold_a, hold_b)
        for t in range(mp):
            for p in range(planes):
                ext[pl.ds(p * lanes + t, SUB, stride=mp), :] = swept[t][p]
        ext[pl.ds(cells, planes, stride=lanes), :] = before
        ext[pl.ds(cells + 1, planes, stride=lanes), :] = (
            pos_buf[step, ipos + 1, 0:planes, :]
            + pos_cbuf[ipos + 1, 0:1, :] * end
            + pos_cbuf[ipos + 1, 1:2, :] * beyond
        )
        for p in range(planes):
            turned[p * width : (p + 1) * width, :] = ext[p * lanes : (p + 1) * lanes, :].T
        source = [
            jnp.stack([turned[pl.ds(p * width + t, SUB, stride=mv), :] for p in range(planes)])
            for t in range(mv)
        ]
        own, outer_own, first, own_end = eliminate(vel_block, source, hold_a, hold_b)
        vel_buf[step, ivel, 0:planes, :] = first
        vel_buf[step, ivel, planes : 2 * planes, :] = own_end
        spread(*vel_args[step])
        if step == 0:
            spread_wait_recv(*vel_coef_args)
            vel_kept = reduced_coefs(vel_cbuf, nvel)
        spread_wait_recv(*vel_args[step])
        reduced_solve(vel_kept, vel_buf, step, vel_whole, nvel, planes)
        before, end, beyond = vel_whole[ivel], vel_whole[ivel + 1], vel_whole[ivel + 2]
        solved = finish(vel_block, own, outer_own, before, end, hold_a, hold_b)
        for t in range(mv):
            for p in range(planes):
                turned[pl.ds(p * width + t, SUB, stride=mv), :] = solved[t][p]
        if step < STEPS - 1:
            for p in range(planes):
                ext[p * lanes : (p + 1) * lanes, :] = turned[p * width : (p + 1) * width, :].T
            field = []
            for t in range(mp):
                keep = 1.0 - mask[pl.ds(t, SUB, stride=mp), :].astype(jnp.float32)
                field.append(
                    jnp.stack(
                        [ext[pl.ds(p * lanes + t, SUB, stride=mp), :] for p in range(planes)]
                    )
                    * keep
                )
            row_before = ext[pl.ds(cells, planes, stride=lanes), :] * keep_before
            row_after = ext[pl.ds(cells + 1, planes, stride=lanes), :] * keep_after
            following = (
                vel_buf[step, ivel + 1, 0:planes, :]
                + vel_cbuf[ivel + 1, 0:1, :] * end
                + vel_cbuf[ivel + 1, 1:2, :] * beyond
            )
            columns = jnp.concatenate([before * col_keep_left, following * col_keep_right], axis=0)
        else:
            keep = 1.0 - mask[...].astype(jnp.float32)
            for p in range(planes):
                result = turned[p * width : (p + 1) * width, :].T
                out[p * cells : (p + 1) * cells, :] = result[0:cells] * keep

    edge_each(0, lambda c, _: c.wait_send())
    edge_each(1, lambda c, _: c.wait_send())
    for args in [pos_coef_args, vel_coef_args] + pos_args + vel_args:
        spread_wait_send(*args)


def on_device(npos, nvel, density, pos_coef, vel_coef, exit_mask, phase_index):
    planes, cells, width = density.shape
    f32 = jnp.float32
    vmem = pl.BlockSpec(memory_space=pltpu.VMEM)
    dma = pltpu.SemaphoreType.DMA
    scratch = lambda *shape: pltpu.VMEM(shape, f32)
    field, absorbed = pl.pallas_call(
        functools.partial(kernel, npos, nvel, planes, cells, width),
        out_shape=(
            jax.ShapeDtypeStruct((planes * cells, width), f32),
            jax.ShapeDtypeStruct((cells, width), f32),
        ),
        in_specs=[vmem] * 4 + [pl.BlockSpec(memory_space=pltpu.SMEM)],
        out_specs=(vmem, vmem),
        scratch_shapes=[
            scratch(planes * 128, width),
            scratch(planes * width, 128),
            scratch(128, width),
            scratch(128, width),
            scratch(16, width),
            scratch(16, width),
            scratch(2, 16, width),
            scratch(2, 16, width),
            scratch(npos + 1, 8, width),
            scratch(nvel + 1, 8, width),
            scratch(STEPS, npos + 1, 2 * planes, width),
            scratch(STEPS, nvel + 1, 2 * planes, width),
            scratch(npos + 2, planes, width),
            scratch(nvel + 2, planes, width),
            scratch(planes * SUB, width),
            scratch(planes * SUB, width),
            dma((2, 2)),
            dma((2, 2)),
            dma((1 + STEPS, npos)),
            dma((1 + STEPS, npos)),
            dma((1 + STEPS, nvel)),
            dma((1 + STEPS, nvel)),
        ],
        compiler_params=pltpu.CompilerParams(
            collective_id=0, has_side_effects=True, vmem_limit_bytes=24 * 1024 * 1024
        ),
        cost_estimate=pl.CostEstimate(
            flops=2_000_000, bytes_accessed=400_000, transcendentals=1024
        ),
        name="line_solves",
    )(density.reshape(planes * cells, width), pos_coef, vel_coef, exit_mask, phase_index)
    return field.reshape(planes, cells, width), absorbed


def solution(mesh):
    return jax.shard_map(
        functools.partial(on_device, mesh.shape["pos"], mesh.shape["vel"]),
        mesh=mesh,
        in_specs=(P(None, "pos", "vel"), P("pos", "vel"), P("pos", "vel"), P("pos", "vel"), P()),
        out_specs=(P(None, "pos", "vel"), P("pos", "vel")),
        check_vma=False,
    )
```

```python
import functools
import math

import jax
import jax.numpy as jnp
from jax import lax
from jax.experimental import pallas as pl
from jax.experimental.pallas import tpu as pltpu
from jax.sharding import PartitionSpec as P

STEPS = 2
NPHASE = 64
SUB = 8
MESH = pl.DeviceIdType.MESH


def coef_chain(low, high, excess):
    inv, carry_low, ups, lows, rest = [], [], [], [], []
    for t in range(len(low)):
        if t == 0:
            left_low, left_rest = low[0], excess[0]
        else:
            left_low, left_rest = low[t] * lows[-1], low[t] * rest[-1] + excess[t]
        factor = 1.0 / (left_low + left_rest + high[t])
        inv.append(factor)
        carry_low.append(low[t] * factor)
        ups.append(high[t] * factor)
        lows.append(left_low * factor)
        rest.append(left_rest * factor)
    beta, gamma, eps = lows[-1], ups[-1], rest[-1]
    betas, gammas, epss = [beta], [gamma], [eps]
    for t in range(len(low) - 2, -1, -1):
        beta = lows[t] + ups[t] * beta
        gamma = ups[t] * gamma
        eps = rest[t] + ups[t] * eps
        betas.append(beta)
        gammas.append(gamma)
        epss.append(eps)
    return inv, carry_low, ups, betas[::-1], gammas[::-1], epss[::-1]


def source_chain(chain, source):
    inv, carry_low, ups = chain[:3]
    forward = [source[0] * inv[0]]
    for t in range(1, len(source)):
        forward.append(source[t] * inv[t] + carry_low[t] * forward[-1])
    own = [forward[-1]]
    for t in range(len(source) - 2, -1, -1):
        own.append(forward[t] + ups[t] * own[-1])
    return own[::-1]


def next_sub(x, axis):
    return pltpu.roll(x, SUB - 1, axis)


def factor_block(coef, store_row):
    one = jnp.ones_like(coef[0])
    inner = coef_chain(coef[:-1], coef[:-1], [one] * (len(coef) - 1))
    beta, gamma, eps = inner[3:]
    last = coef[-1]
    low = last * beta[-1]
    high = last * next_sub(gamma[0], 0)
    excess = 1.0 + last * eps[-1] + last * next_sub(eps[0], 0)
    rows = lambda x: [x[s : s + 1] for s in range(SUB - 1)]
    outer = coef_chain(rows(low), rows(high), rows(excess))
    obeta, ogamma, oeps = outer[3:]
    end = slice(SUB - 1, SUB)
    first_gamma = gamma[0][0:1]
    store_row(0, beta[0][0:1] + first_gamma * obeta[0])
    store_row(1, first_gamma * ogamma[0])
    store_row(2, eps[0][0:1] + first_gamma * oeps[0])
    store_row(3, last[end])
    store_row(4, low[end] * obeta[-1])
    store_row(5, 1.0 + last[end] * eps[-1][end] + low[end] * oeps[-1])
    return inner, outer, last, first_gamma, low[end]


def eliminate(block, source, hold_a, hold_b):
    inner, outer, last, first_gamma, end_low = block
    planes = source[0].shape[0]
    own = source_chain(inner, source[:-1])
    sub = lax.broadcasted_iota(jnp.int32, source[0].shape, 1)
    after = jnp.where(sub == SUB - 1, 0.0, next_sub(own[0], 1))
    seps = source[-1] + last * (own[-1] + after)
    hold_a[...] = seps.reshape(hold_a.shape)
    hold_b[...] = own[0].reshape(hold_b.shape)
    row = lambda ref, s: ref[pl.ds(s, planes, stride=SUB), :]
    outer_own = source_chain(outer, [row(hold_a, s) for s in range(SUB - 1)])
    first = row(hold_b, 0) + first_gamma * outer_own[0]
    own_end = row(hold_a, SUB - 1) + end_low * outer_own[-1]
    return own, outer_own, first, own_end


def finish(block, own, outer_own, before, end, hold_a, hold_b):
    inner, outer = block[:2]
    planes = before.shape[0]
    hold_b[pl.ds(0, planes, stride=SUB), :] = before
    for s in range(SUB - 1):
        value = outer_own[s] + outer[3][s] * before + outer[4][s] * end
        hold_a[pl.ds(s, planes, stride=SUB), :] = value
        hold_b[pl.ds(s + 1, planes, stride=SUB), :] = value
    hold_a[pl.ds(SUB - 1, planes, stride=SUB), :] = end
    right = hold_a[...].reshape(own[0].shape)
    left = hold_b[...].reshape(own[0].shape)
    return [p + b * left + g * right for p, b, g in zip(own, inner[3], inner[4])] + [right]


def reduced_coefs(buf, count):
    kept, rest = [], 1.0
    for d in range(count):
        link = buf[d, 3:4, :]
        left = buf[d, 4:5, :]
        high = link * buf[d + 1, 1:2, :]
        excess = left * rest + buf[d, 5:6, :] + link * buf[d + 1, 2:3, :]
        factor = 1.0 / (excess + high)
        rest = excess * factor
        kept.append((factor, left * factor, high * factor, link * factor))
    return kept


def reduced_solve(kept, buf, step, whole, count, planes):
    forward, prior = [], None
    for d in range(count):
        factor, left, _, link = kept[d]
        value = factor * buf[step, d, planes : 2 * planes, :] + link * buf[step, d + 1, 0:planes, :]
        prior = value if prior is None else value + left * prior
        forward.append(prior)
    value = forward[-1]
    whole[count] = value
    for d in range(count - 2, -1, -1):
        value = forward[d] + kept[d][2] * value
        whole[d + 1] = value


def kernel(
    npos, nvel, planes, cells, width,
    dens_in, pcoef_in, vcoef_in, mask_in, phase_in,
    out, taken,
    dens, pcoef, vcoef, mask, phase, rates_up, rates_down,
    ext, turned, edge_tmp, vext, pos_edge, vel_edge, pos_edge_in, vel_edge_in,
    pos_cbuf, vel_cbuf, pos_buf, vel_buf, pos_whole, vel_whole, hold_a, hold_b,
    load_sem, edge_send, edge_recv, psend, precv, vsend, vrecv,
):
    lanes = width
    mp, mv = cells // SUB, width // SUB
    ipos, ivel = lax.axis_index("pos"), lax.axis_index("vel")

    pos_id = lambda d: (d, ivel)
    vel_id = lambda d: (ipos, d)

    barrier = pltpu.get_barrier_semaphore()

    def greet(count, me, ident):
        for off in range(1, count):
            peer = lax.rem(me + off, count)
            pl.semaphore_signal(barrier, 1, device_id=ident(peer), device_id_type=MESH)

    loads = [
        pltpu.make_async_copy(src, dst, load_sem.at[i])
        for i, (src, dst) in enumerate(
            (
                (dens_in, dens),
                (mask_in, mask),
                (vcoef_in, vcoef),
                (pcoef_in, pcoef),
                (phase_in, phase),
            )
        )
    ]
    pos_edge_in[...] = jnp.zeros_like(pos_edge_in)
    vel_edge_in[...] = jnp.zeros_like(vel_edge_in)
    greet(npos, ipos, pos_id)
    greet(nvel, ivel, vel_id)
    for load in loads:
        load.start()
    ext[...] = jnp.zeros_like(ext)
    vext[...] = jnp.zeros_like(vext)
    edge_tmp[...] = jnp.zeros_like(edge_tmp)
    for cbuf, buf, whole, count in (
        (pos_cbuf, pos_buf, pos_whole, npos),
        (vel_cbuf, vel_buf, vel_whole, nvel),
    ):
        sub = lax.broadcasted_iota(jnp.int32, (8, lanes), 0)
        cbuf[count] = jnp.where(sub == 2, 1.0, 0.0)
        buf[0, count] = jnp.zeros((2 * planes, lanes), jnp.float32)
        buf[1, count] = jnp.zeros((2 * planes, lanes), jnp.float32)
        whole[0] = jnp.zeros((planes, lanes), jnp.float32)
        whole[count + 1] = jnp.zeros((planes, lanes), jnp.float32)

    for load in loads:
        load.wait()

    hit = mask[...].astype(jnp.float32)
    pos_edge[...] = jnp.zeros_like(pos_edge)
    for p in range(planes):
        pos_edge[p : p + 1, :] = dens[p * cells : p * cells + 1, :]
        pos_edge[planes + p : planes + p + 1, :] = dens[(p + 1) * cells - 1 : (p + 1) * cells, :]
    pos_edge[2 * planes : 2 * planes + 1, :] = hit[0:1]
    pos_edge[2 * planes + 1 : 2 * planes + 2, :] = hit[cells - 1 : cells]
    pos_edge[2 * planes + 2 : 2 * planes + 3, :] = vcoef[0:1, :]
    pos_edge[2 * planes + 3 : 2 * planes + 4, :] = vcoef[cells - 1 : cells, :]
    lane = lax.broadcasted_iota(jnp.int32, (cells, lanes), 1)
    gathered = jnp.zeros((cells, lanes), jnp.float32)
    for p in range(planes):
        one = dens[p * cells : (p + 1) * cells, :]
        gathered = jnp.where(lane == p, one[:, 0:1], gathered)
        gathered = jnp.where(lane == planes + p, one[:, lanes - 1 : lanes], gathered)
    gathered = jnp.where(lane == 2 * planes, hit[:, 0:1], gathered)
    gathered = jnp.where(lane == 2 * planes + 1, hit[:, lanes - 1 : lanes], gathered)
    edge_tmp[0:cells, :] = gathered
    vel_edge[...] = edge_tmp[...].T[0:16]

    def edge_copy(axis, to_right, src, dst, ident, me):
        slot = 0 if to_right else 1
        peer = me + 1 if to_right else me - 1
        return pltpu.make_async_remote_copy(
            src_ref=src, dst_ref=dst.at[slot],
            send_sem=edge_send.at[axis, slot], recv_sem=edge_recv.at[axis, slot],
            device_id=ident(peer), device_id_type=MESH,
        )

    sides = (
        (0, pos_edge, pos_edge_in, pos_id, ipos, npos),
        (1, vel_edge, vel_edge_in, vel_id, ivel, nvel),
    )

    def edge_each(which, act):
        axis, src, dst, ident, me, count = sides[which]

        @pl.when(me < count - 1)
        def _():
            act(edge_copy(axis, True, src, dst, ident, me), True)

        @pl.when(me > 0)
        def _():
            act(edge_copy(axis, False, src, dst, ident, me), False)

    def edge_wait(which):
        axis, src, dst, ident, me, count = sides[which]

        @pl.when(me > 0)
        def _():
            edge_copy(axis, True, src, dst, ident, me).wait_recv()

        @pl.when(me < count - 1)
        def _():
            edge_copy(axis, False, src, dst, ident, me).wait_recv()

    def spread_copy(ref, kind, sends, recvs, ident, me, count, off):
        peer = lax.rem(me + off, count)
        return pltpu.make_async_remote_copy(
            src_ref=ref.at[me], dst_ref=ref.at[me],
            send_sem=sends.at[kind, off], recv_sem=recvs.at[kind, me],
            device_id=ident(peer), device_id_type=MESH,
        )

    def spread(*args):
        for off in range(1, args[-1]):
            spread_copy(*args, off).start()

    def spread_wait_recv(ref, kind, sends, recvs, ident, me, count):
        for off in range(1, count):
            sender = lax.rem(me + off, count)
            pltpu.make_async_remote_copy(
                src_ref=ref.at[sender], dst_ref=ref.at[sender],
                send_sem=sends.at[kind, off], recv_sem=recvs.at[kind, sender],
                device_id=ident(sender), device_id_type=MESH,
            ).wait_recv()

    def spread_wait_send(*args):
        for off in range(1, args[-1]):
            spread_copy(*args, off).wait_send()

    pos_coef_args = (pos_cbuf, 0, psend, precv, pos_id, ipos, npos)
    vel_coef_args = (vel_cbuf, 0, vsend, vrecv, vel_id, ivel, nvel)
    pos_args = [(pos_buf.at[i], 1 + i, psend, precv, pos_id, ipos, npos) for i in range(STEPS)]
    vel_args = [(vel_buf.at[i], 1 + i, vsend, vrecv, vel_id, ivel, nvel) for i in range(STEPS)]

    pos_cbuf[ipos] = jnp.zeros((8, lanes), jnp.float32)

    def pos_row(r, value):
        pos_cbuf[ipos, r : r + 1, :] = value

    pos_block = factor_block([pcoef[pl.ds(t, SUB, stride=mp), :] for t in range(mp)], pos_row)
    sub = lax.broadcasted_iota(jnp.int32, (SUB, lanes), 0)
    lane = lax.broadcasted_iota(jnp.int32, (SUB, lanes), 1)
    turns = jnp.zeros((SUB, lanes), jnp.int32)
    for p in range(planes):
        turns = jnp.where(sub == p, phase[p], turns)
    cosine = 0.6 * jnp.cos(2.0 * math.pi * turns.astype(jnp.float32) / NPHASE)
    vpos = (2.0 * (ivel * width + lane).astype(jnp.float32) + 1.0) * (1.0 / (width * nvel)) - 1.0
    move = 0.45 * vpos
    move_up, move_down = jnp.maximum(move, 0.0), jnp.minimum(move, 0.0)
    cosines = jnp.stack([jnp.broadcast_to(cosine[p : p + 1], (SUB, lanes)) for p in range(planes)])

    for t in range(mp):
        xpos = 1.5 * (
            (2.0 * (ipos * cells + sub * mp + t).astype(jnp.float32) + 1.0) * (1.0 / (cells * npos))
            - 1.0
        )
        rate = 0.15 * (((xpos - xpos * xpos * xpos)[None] + cosines) - (0.5 * vpos)[None])
        rates_up[t] = jnp.maximum(rate, 0.0)
        rates_down[t] = jnp.minimum(rate, 0.0)

    pl.semaphore_wait(barrier, (npos - 1) + (nvel - 1))

    edge_each(0, lambda c, _: c.start())
    edge_each(1, lambda c, _: c.start())
    spread(*pos_coef_args)

    def drift(step, field, row_before, row_after, columns):
        edge_tmp[0 : 2 * planes, :] = columns
        if step > 0:
            edge_tmp[2 * planes : 16, :] = jnp.zeros((16 - 2 * planes, lanes), jnp.float32)
        turned[0:lanes, :] = edge_tmp[...].T
        wide_sub = lax.broadcasted_iota(jnp.int32, (planes, SUB, lanes), 1)
        wide_lane = lax.broadcasted_iota(jnp.int32, (planes, SUB, lanes), 2)
        before = jnp.where(wide_sub == 0, row_before[:, None, :], pltpu.roll(field[-1], 1, 1))
        after = jnp.where(wide_sub == SUB - 1, row_after[:, None, :], next_sub(field[0], 1))
        kept = []
        for t in range(mp):
            center = field[t]
            back = field[t - 1] if t else before
            ahead = field[t + 1] if t < mp - 1 else after
            cols = turned[pl.ds(t, SUB, stride=mp), :]
            left = jnp.stack([cols[:, p : p + 1] for p in range(planes)])
            right = jnp.stack([cols[:, planes + p : planes + p + 1] for p in range(planes)])
            back_v = jnp.where(wide_lane == 0, left, pltpu.roll(center, 1, 2))
            ahead_v = jnp.where(wide_lane == lanes - 1, right, pltpu.roll(center, lanes - 1, 2))
            along_x = move_up * (center - back) + move_down * (ahead - center)
            along_v = rates_up[t] * (center - back_v) + rates_down[t] * (ahead_v - center)
            drifted = center - along_x - along_v
            hit_t = mask[pl.ds(t, SUB, stride=mp), :].astype(jnp.float32)
            took = jnp.sum(drifted, axis=0) * hit_t
            if step > 0:
                took = taken[pl.ds(t, SUB, stride=mp), :] + took
            taken[pl.ds(t, SUB, stride=mp), :] = took
            kept.append(drifted * (1.0 - hit_t))
        return kept

    edge_wait(1)
    edge_wait(0)
    row_before = pos_edge_in[0, planes : 2 * planes, :]
    row_after = pos_edge_in[1, 0:planes, :]
    keep_before = 1.0 - pos_edge_in[0, 2 * planes + 1 : 2 * planes + 2, :]
    keep_after = 1.0 - pos_edge_in[1, 2 * planes : 2 * planes + 1, :]
    col_keep_left = 1.0 - vel_edge_in[0, 2 * planes + 1 : 2 * planes + 2, :]
    col_keep_right = 1.0 - vel_edge_in[1, 2 * planes : 2 * planes + 1, :]
    columns = jnp.concatenate(
        [vel_edge_in[0, planes : 2 * planes, :], vel_edge_in[1, 0:planes, :]], axis=0
    )
    field = [
        jnp.stack([dens[pl.ds(p * cells + t, SUB, stride=mp), :] for p in range(planes)])
        for t in range(mp)
    ]
    vel_block = pos_kept = vel_kept = None

    for step in range(STEPS):
        kept = drift(step, field, row_before, row_after, columns)
        own, outer_own, first, own_end = eliminate(pos_block, kept, hold_a, hold_b)
        pos_buf[step, ipos, 0:planes, :] = first
        pos_buf[step, ipos, planes : 2 * planes, :] = own_end
        spread(*pos_args[step])
        if step == 0:
            vext[0:cells, :] = vcoef[...]
            vext[cells : cells + 1, :] = pos_edge_in[0, 2 * planes + 3 : 2 * planes + 4, :]
            vext[cells + 1 : cells + 2, :] = pos_edge_in[1, 2 * planes + 2 : 2 * planes + 3, :]
            turned[0:width, :] = vext[...].T
            vel_cbuf[ivel] = jnp.zeros((8, lanes), jnp.float32)

            def vel_row(r, value):
                vel_cbuf[ivel, r : r + 1, :] = value

            vel_block = factor_block(
                [turned[pl.ds(t, SUB, stride=mv), :] for t in range(mv)], vel_row
            )
            spread(*vel_coef_args)
            spread_wait_recv(*pos_coef_args)
            pos_kept = reduced_coefs(pos_cbuf, npos)
        spread_wait_recv(*pos_args[step])
        reduced_solve(pos_kept, pos_buf, step, pos_whole, npos, planes)
        before, end, beyond = pos_whole[ipos], pos_whole[ipos + 1], pos_whole[ipos + 2]
        swept = finish(pos_block, own, outer_own, before, end, hold_a, hold_b)
        for t in range(mp):
            for p in range(planes):
                ext[pl.ds(p * lanes + t, SUB, stride=mp), :] = swept[t][p]
        ext[pl.ds(cells, planes, stride=lanes), :] = before
        ext[pl.ds(cells + 1, planes, stride=lanes), :] = (
            pos_buf[step, ipos + 1, 0:planes, :]
            + pos_cbuf[ipos + 1, 0:1, :] * end
            + pos_cbuf[ipos + 1, 1:2, :] * beyond
        )
        for p in range(planes):
            turned[p * width : (p + 1) * width, :] = ext[p * lanes : (p + 1) * lanes, :].T
        source = [
            jnp.stack([turned[pl.ds(p * width + t, SUB, stride=mv), :] for p in range(planes)])
            for t in range(mv)
        ]
        own, outer_own, first, own_end = eliminate(vel_block, source, hold_a, hold_b)
        vel_buf[step, ivel, 0:planes, :] = first
        vel_buf[step, ivel, planes : 2 * planes, :] = own_end
        spread(*vel_args[step])
        if step == 0:
            spread_wait_recv(*vel_coef_args)
            vel_kept = reduced_coefs(vel_cbuf, nvel)
        spread_wait_recv(*vel_args[step])
        reduced_solve(vel_kept, vel_buf, step, vel_whole, nvel, planes)
        before, end, beyond = vel_whole[ivel], vel_whole[ivel + 1], vel_whole[ivel + 2]
        solved = finish(vel_block, own, outer_own, before, end, hold_a, hold_b)
        for t in range(mv):
            for p in range(planes):
                turned[pl.ds(p * width + t, SUB, stride=mv), :] = solved[t][p]
        if step < STEPS - 1:
            for p in range(planes):
                ext[p * lanes : (p + 1) * lanes, :] = turned[p * width : (p + 1) * width, :].T
            field = []
            for t in range(mp):
                keep = 1.0 - mask[pl.ds(t, SUB, stride=mp), :].astype(jnp.float32)
                field.append(
                    jnp.stack(
                        [ext[pl.ds(p * lanes + t, SUB, stride=mp), :] for p in range(planes)]
                    )
                    * keep
                )
            row_before = ext[pl.ds(cells, planes, stride=lanes), :] * keep_before
            row_after = ext[pl.ds(cells + 1, planes, stride=lanes), :] * keep_after
            following = (
                vel_buf[step, ivel + 1, 0:planes, :]
                + vel_cbuf[ivel + 1, 0:1, :] * end
                + vel_cbuf[ivel + 1, 1:2, :] * beyond
            )
            columns = jnp.concatenate([before * col_keep_left, following * col_keep_right], axis=0)
        else:
            keep = 1.0 - mask[...].astype(jnp.float32)
            for p in range(planes):
                result = turned[p * width : (p + 1) * width, :].T
                out[p * cells : (p + 1) * cells, :] = result[0:cells] * keep

    edge_each(0, lambda c, _: c.wait_send())
    edge_each(1, lambda c, _: c.wait_send())
    for args in [pos_coef_args, vel_coef_args] + pos_args + vel_args:
        spread_wait_send(*args)


def on_device(npos, nvel, density, pos_coef, vel_coef, exit_mask, phase_index):
    planes, cells, width = density.shape
    f32 = jnp.float32
    vmem = pl.BlockSpec(memory_space=pltpu.VMEM)
    dma = pltpu.SemaphoreType.DMA
    scratch = lambda *shape: pltpu.VMEM(shape, f32)
    field, absorbed = pl.pallas_call(
        functools.partial(kernel, npos, nvel, planes, cells, width),
        out_shape=(
            pltpu.VMEM((planes * cells, width), f32),
            pltpu.VMEM((cells, width), f32),
        ),
        in_specs=[pl.BlockSpec(memory_space=pltpu.HBM)] * 5,
        out_specs=(vmem, vmem),
        scratch_shapes=[
            scratch(planes * cells, width),
            scratch(cells, width),
            scratch(cells, width),
            pltpu.VMEM((cells, width), jnp.int32),
            pltpu.SMEM((planes,), jnp.int32),
            scratch(cells // SUB, planes, SUB, width),
            scratch(cells // SUB, planes, SUB, width),
            scratch(planes * 128, width),
            scratch(planes * width, 128),
            scratch(128, width),
            scratch(128, width),
            scratch(16, width),
            scratch(16, width),
            scratch(2, 16, width),
            scratch(2, 16, width),
            scratch(npos + 1, 8, width),
            scratch(nvel + 1, 8, width),
            scratch(STEPS, npos + 1, 2 * planes, width),
            scratch(STEPS, nvel + 1, 2 * planes, width),
            scratch(npos + 2, planes, width),
            scratch(nvel + 2, planes, width),
            scratch(planes * SUB, width),
            scratch(planes * SUB, width),
            dma((5,)),
            dma((2, 2)),
            dma((2, 2)),
            dma((1 + STEPS, npos)),
            dma((1 + STEPS, npos)),
            dma((1 + STEPS, nvel)),
            dma((1 + STEPS, nvel)),
        ],
        compiler_params=pltpu.CompilerParams(
            collective_id=0, has_side_effects=True
        ),
        cost_estimate=pl.CostEstimate(
            flops=2_000_000, bytes_accessed=400_000, transcendentals=1024
        ),
        name="line_solves",
    )(density.reshape(planes * cells, width), pos_coef, vel_coef, exit_mask, phase_index)
    return field.reshape(planes, cells, width), absorbed


def solution(mesh):
    return jax.shard_map(
        functools.partial(on_device, mesh.shape["pos"], mesh.shape["vel"]),
        mesh=mesh,
        in_specs=(P(None, "pos", "vel"), P("pos", "vel"), P("pos", "vel"), P("pos", "vel"), P()),
        out_specs=(P(None, "pos", "vel"), P("pos", "vel")),
        check_vma=False,
    )
```

```python
import functools
import math

import jax
import jax.numpy as jnp
from jax import lax
from jax.experimental import pallas as pl
from jax.experimental.pallas import tpu as pltpu
from jax.sharding import PartitionSpec as P

STEPS = 2
NPHASE = 64
SUB = 8
MESH = pl.DeviceIdType.MESH


def coef_chain(low, high, excess):
    inv, carry_low, ups, lows, rest = [], [], [], [], []
    for t in range(len(low)):
        if t == 0:
            left_low, left_rest = low[0], excess[0]
        else:
            left_low, left_rest = low[t] * lows[-1], low[t] * rest[-1] + excess[t]
        factor = 1.0 / (left_low + left_rest + high[t])
        inv.append(factor)
        carry_low.append(low[t] * factor)
        ups.append(high[t] * factor)
        lows.append(left_low * factor)
        rest.append(left_rest * factor)
    beta, gamma, eps = lows[-1], ups[-1], rest[-1]
    betas, gammas, epss = [beta], [gamma], [eps]
    for t in range(len(low) - 2, -1, -1):
        beta = lows[t] + ups[t] * beta
        gamma = ups[t] * gamma
        eps = rest[t] + ups[t] * eps
        betas.append(beta)
        gammas.append(gamma)
        epss.append(eps)
    return inv, carry_low, ups, betas[::-1], gammas[::-1], epss[::-1]


def source_chain(chain, source):
    inv, carry_low, ups = chain[:3]
    forward = [source[0] * inv[0]]
    for t in range(1, len(source)):
        forward.append(source[t] * inv[t] + carry_low[t] * forward[-1])
    own = [forward[-1]]
    for t in range(len(source) - 2, -1, -1):
        own.append(forward[t] + ups[t] * own[-1])
    return own[::-1]


def next_sub(x, axis):
    return pltpu.roll(x, SUB - 1, axis)


def factor_block(coef, store_row):
    one = jnp.ones_like(coef[0])
    inner = coef_chain(coef[:-1], coef[:-1], [one] * (len(coef) - 1))
    beta, gamma, eps = inner[3:]
    last = coef[-1]
    low = last * beta[-1]
    high = last * next_sub(gamma[0], 0)
    excess = 1.0 + last * eps[-1] + last * next_sub(eps[0], 0)
    rows = lambda x: [x[s : s + 1] for s in range(SUB - 1)]
    outer = coef_chain(rows(low), rows(high), rows(excess))
    obeta, ogamma, oeps = outer[3:]
    end = slice(SUB - 1, SUB)
    first_gamma = gamma[0][0:1]
    store_row(0, beta[0][0:1] + first_gamma * obeta[0])
    store_row(1, first_gamma * ogamma[0])
    store_row(2, eps[0][0:1] + first_gamma * oeps[0])
    store_row(3, last[end])
    store_row(4, low[end] * obeta[-1])
    store_row(5, 1.0 + last[end] * eps[-1][end] + low[end] * oeps[-1])
    return inner, outer, last, first_gamma, low[end]


def eliminate(block, source, hold_a, hold_b):
    inner, outer, last, first_gamma, end_low = block
    planes = source[0].shape[0]
    own = source_chain(inner, source[:-1])
    sub = lax.broadcasted_iota(jnp.int32, source[0].shape, 1)
    after = jnp.where(sub == SUB - 1, 0.0, next_sub(own[0], 1))
    seps = source[-1] + last * (own[-1] + after)
    hold_a[...] = seps.reshape(hold_a.shape)
    hold_b[...] = own[0].reshape(hold_b.shape)
    row = lambda ref, s: ref[pl.ds(s, planes, stride=SUB), :]
    outer_own = source_chain(outer, [row(hold_a, s) for s in range(SUB - 1)])
    first = row(hold_b, 0) + first_gamma * outer_own[0]
    own_end = row(hold_a, SUB - 1) + end_low * outer_own[-1]
    return own, outer_own, first, own_end


def finish(block, own, outer_own, before, end, hold_a, hold_b):
    inner, outer = block[:2]
    planes = before.shape[0]
    hold_b[pl.ds(0, planes, stride=SUB), :] = before
    for s in range(SUB - 1):
        value = outer_own[s] + outer[3][s] * before + outer[4][s] * end
        hold_a[pl.ds(s, planes, stride=SUB), :] = value
        hold_b[pl.ds(s + 1, planes, stride=SUB), :] = value
    hold_a[pl.ds(SUB - 1, planes, stride=SUB), :] = end
    right = hold_a[...].reshape(own[0].shape)
    left = hold_b[...].reshape(own[0].shape)
    return [p + b * left + g * right for p, b, g in zip(own, inner[3], inner[4])] + [right]


def reduced_coefs(buf, count):
    kept, rest = [], 1.0
    for d in range(count):
        link = buf[d, 3:4, :]
        left = buf[d, 4:5, :]
        high = link * buf[d + 1, 1:2, :]
        excess = left * rest + buf[d, 5:6, :] + link * buf[d + 1, 2:3, :]
        factor = 1.0 / (excess + high)
        rest = excess * factor
        kept.append((factor, left * factor, high * factor, link * factor))
    return kept


def reduced_solve(kept, buf, step, whole, count, planes):
    forward, prior = [], None
    for d in range(count):
        factor, left, _, link = kept[d]
        value = factor * buf[step, d, planes : 2 * planes, :] + link * buf[step, d + 1, 0:planes, :]
        prior = value if prior is None else value + left * prior
        forward.append(prior)
    value = forward[-1]
    whole[count] = value
    for d in range(count - 2, -1, -1):
        value = forward[d] + kept[d][2] * value
        whole[d + 1] = value


def kernel(
    npos, nvel, planes, cells, width,
    dens_in, pcoef_in, vcoef_in, mask_in, phase_in,
    out, taken,
    dens, pcoef, vcoef, mask, phase, rates_up, rates_down,
    ext, turned, edge_tmp, vext, pos_edge, vel_edge, pos_edge_in, vel_edge_in,
    pos_cbuf, vel_cbuf, pos_buf, vel_buf, pos_whole, vel_whole, hold_a, hold_b,
    load_sem, edge_send, edge_recv, psend, precv, vsend, vrecv,
):
    lanes = width
    mp, mv = cells // SUB, width // SUB
    ipos, ivel = lax.axis_index("pos"), lax.axis_index("vel")

    pos_id = lambda d: (d, ivel)
    vel_id = lambda d: (ipos, d)

    barrier = pltpu.get_barrier_semaphore()

    def greet(count, me, ident):
        for off in range(1, count):
            peer = lax.rem(me + off, count)
            pl.semaphore_signal(barrier, 1, device_id=ident(peer), device_id_type=MESH)

    loads = [
        pltpu.make_async_copy(src, dst, load_sem.at[i])
        for i, (src, dst) in enumerate(
            (
                (dens_in, dens),
                (mask_in, mask),
                (vcoef_in, vcoef),
                (pcoef_in, pcoef),
                (phase_in, phase),
            )
        )
    ]
    pos_edge_in[...] = jnp.zeros_like(pos_edge_in)
    vel_edge_in[...] = jnp.zeros_like(vel_edge_in)
    greet(npos, ipos, pos_id)
    greet(nvel, ivel, vel_id)
    for load in loads:
        load.start()
    ext[...] = jnp.zeros_like(ext)
    vext[...] = jnp.zeros_like(vext)
    edge_tmp[...] = jnp.zeros_like(edge_tmp)
    for cbuf, buf, whole, count in (
        (pos_cbuf, pos_buf, pos_whole, npos),
        (vel_cbuf, vel_buf, vel_whole, nvel),
    ):
        sub = lax.broadcasted_iota(jnp.int32, (8, lanes), 0)
        cbuf[count] = jnp.where(sub == 2, 1.0, 0.0)
        buf[0, count] = jnp.zeros((2 * planes, lanes), jnp.float32)
        buf[1, count] = jnp.zeros((2 * planes, lanes), jnp.float32)
        whole[0] = jnp.zeros((planes, lanes), jnp.float32)
        whole[count + 1] = jnp.zeros((planes, lanes), jnp.float32)

    for load in loads[:3]:
        load.wait()

    hit = mask[...].astype(jnp.float32)
    pos_edge[...] = jnp.zeros_like(pos_edge)
    for p in range(planes):
        pos_edge[p : p + 1, :] = dens[p * cells : p * cells + 1, :]
        pos_edge[planes + p : planes + p + 1, :] = dens[(p + 1) * cells - 1 : (p + 1) * cells, :]
    pos_edge[2 * planes : 2 * planes + 1, :] = hit[0:1]
    pos_edge[2 * planes + 1 : 2 * planes + 2, :] = hit[cells - 1 : cells]
    pos_edge[2 * planes + 2 : 2 * planes + 3, :] = vcoef[0:1, :]
    pos_edge[2 * planes + 3 : 2 * planes + 4, :] = vcoef[cells - 1 : cells, :]
    lane = lax.broadcasted_iota(jnp.int32, (cells, lanes), 1)
    gathered = jnp.zeros((cells, lanes), jnp.float32)
    for p in range(planes):
        one = dens[p * cells : (p + 1) * cells, :]
        gathered = jnp.where(lane == p, one[:, 0:1], gathered)
        gathered = jnp.where(lane == planes + p, one[:, lanes - 1 : lanes], gathered)
    gathered = jnp.where(lane == 2 * planes, hit[:, 0:1], gathered)
    gathered = jnp.where(lane == 2 * planes + 1, hit[:, lanes - 1 : lanes], gathered)
    edge_tmp[0:cells, :] = gathered
    vel_edge[...] = edge_tmp[...].T[0:16]

    def edge_copy(axis, to_right, src, dst, ident, me):
        slot = 0 if to_right else 1
        peer = me + 1 if to_right else me - 1
        return pltpu.make_async_remote_copy(
            src_ref=src, dst_ref=dst.at[slot],
            send_sem=edge_send.at[axis, slot], recv_sem=edge_recv.at[axis, slot],
            device_id=ident(peer), device_id_type=MESH,
        )

    sides = (
        (0, pos_edge, pos_edge_in, pos_id, ipos, npos),
        (1, vel_edge, vel_edge_in, vel_id, ivel, nvel),
    )

    def edge_each(which, act):
        axis, src, dst, ident, me, count = sides[which]

        @pl.when(me < count - 1)
        def _():
            act(edge_copy(axis, True, src, dst, ident, me), True)

        @pl.when(me > 0)
        def _():
            act(edge_copy(axis, False, src, dst, ident, me), False)

    def edge_wait(which):
        axis, src, dst, ident, me, count = sides[which]

        @pl.when(me > 0)
        def _():
            edge_copy(axis, True, src, dst, ident, me).wait_recv()

        @pl.when(me < count - 1)
        def _():
            edge_copy(axis, False, src, dst, ident, me).wait_recv()

    def spread_copy(ref, kind, sends, recvs, ident, me, count, off):
        peer = lax.rem(me + off, count)
        return pltpu.make_async_remote_copy(
            src_ref=ref.at[me], dst_ref=ref.at[me],
            send_sem=sends.at[kind, off], recv_sem=recvs.at[kind, me],
            device_id=ident(peer), device_id_type=MESH,
        )

    def spread(*args):
        for off in range(1, args[-1]):
            spread_copy(*args, off).start()

    def spread_wait_recv(ref, kind, sends, recvs, ident, me, count):
        for off in range(1, count):
            sender = lax.rem(me + off, count)
            pltpu.make_async_remote_copy(
                src_ref=ref.at[sender], dst_ref=ref.at[sender],
                send_sem=sends.at[kind, off], recv_sem=recvs.at[kind, sender],
                device_id=ident(sender), device_id_type=MESH,
            ).wait_recv()

    def spread_wait_send(*args):
        for off in range(1, args[-1]):
            spread_copy(*args, off).wait_send()

    pos_coef_args = (pos_cbuf, 0, psend, precv, pos_id, ipos, npos)
    vel_coef_args = (vel_cbuf, 0, vsend, vrecv, vel_id, ivel, nvel)
    pos_args = [(pos_buf.at[i], 1 + i, psend, precv, pos_id, ipos, npos) for i in range(STEPS)]
    vel_args = [(vel_buf.at[i], 1 + i, vsend, vrecv, vel_id, ivel, nvel) for i in range(STEPS)]

    pl.semaphore_wait(barrier, (npos - 1) + (nvel - 1))
    edge_each(0, lambda c, _: c.start())
    edge_each(1, lambda c, _: c.start())

    for load in loads[3:]:
        load.wait()
    pos_cbuf[ipos] = jnp.zeros((8, lanes), jnp.float32)

    def pos_row(r, value):
        pos_cbuf[ipos, r : r + 1, :] = value

    pos_block = factor_block([pcoef[pl.ds(t, SUB, stride=mp), :] for t in range(mp)], pos_row)
    spread(*pos_coef_args)

    sub = lax.broadcasted_iota(jnp.int32, (SUB, lanes), 0)
    lane = lax.broadcasted_iota(jnp.int32, (SUB, lanes), 1)
    turns = jnp.zeros((SUB, lanes), jnp.int32)
    for p in range(planes):
        turns = jnp.where(sub == p, phase[p], turns)
    cosine = 0.6 * jnp.cos(2.0 * math.pi * turns.astype(jnp.float32) / NPHASE)
    vpos = (2.0 * (ivel * width + lane).astype(jnp.float32) + 1.0) * (1.0 / (width * nvel)) - 1.0
    move = 0.45 * vpos
    move_up, move_down = jnp.maximum(move, 0.0), jnp.minimum(move, 0.0)
    cosines = jnp.stack([jnp.broadcast_to(cosine[p : p + 1], (SUB, lanes)) for p in range(planes)])

    for t in range(mp):
        xpos = 1.5 * (
            (2.0 * (ipos * cells + sub * mp + t).astype(jnp.float32) + 1.0) * (1.0 / (cells * npos))
            - 1.0
        )
        rate = 0.15 * (((xpos - xpos * xpos * xpos)[None] + cosines) - (0.5 * vpos)[None])
        rates_up[t] = jnp.maximum(rate, 0.0)
        rates_down[t] = jnp.minimum(rate, 0.0)

    def drift(step, field, row_before, row_after, columns):
        edge_tmp[0 : 2 * planes, :] = columns
        if step > 0:
            edge_tmp[2 * planes : 16, :] = jnp.zeros((16 - 2 * planes, lanes), jnp.float32)
        turned[0:lanes, :] = edge_tmp[...].T
        wide_sub = lax.broadcasted_iota(jnp.int32, (planes, SUB, lanes), 1)
        wide_lane = lax.broadcasted_iota(jnp.int32, (planes, SUB, lanes), 2)
        before = jnp.where(wide_sub == 0, row_before[:, None, :], pltpu.roll(field[-1], 1, 1))
        after = jnp.where(wide_sub == SUB - 1, row_after[:, None, :], next_sub(field[0], 1))
        kept = []
        for t in range(mp):
            center = field[t]
            back = field[t - 1] if t else before
            ahead = field[t + 1] if t < mp - 1 else after
            cols = turned[pl.ds(t, SUB, stride=mp), :]
            left = jnp.stack([cols[:, p : p + 1] for p in range(planes)])
            right = jnp.stack([cols[:, planes + p : planes + p + 1] for p in range(planes)])
            back_v = jnp.where(wide_lane == 0, left, pltpu.roll(center, 1, 2))
            ahead_v = jnp.where(wide_lane == lanes - 1, right, pltpu.roll(center, lanes - 1, 2))
            along_x = move_up * (center - back) + move_down * (ahead - center)
            along_v = rates_up[t] * (center - back_v) + rates_down[t] * (ahead_v - center)
            drifted = center - along_x - along_v
            hit_t = mask[pl.ds(t, SUB, stride=mp), :].astype(jnp.float32)
            took = jnp.sum(drifted, axis=0) * hit_t
            if step > 0:
                took = taken[pl.ds(t, SUB, stride=mp), :] + took
            taken[pl.ds(t, SUB, stride=mp), :] = took
            kept.append(drifted * (1.0 - hit_t))
        return kept

    edge_wait(1)
    edge_wait(0)
    row_before = pos_edge_in[0, planes : 2 * planes, :]
    row_after = pos_edge_in[1, 0:planes, :]
    keep_before = 1.0 - pos_edge_in[0, 2 * planes + 1 : 2 * planes + 2, :]
    keep_after = 1.0 - pos_edge_in[1, 2 * planes : 2 * planes + 1, :]
    col_keep_left = 1.0 - vel_edge_in[0, 2 * planes + 1 : 2 * planes + 2, :]
    col_keep_right = 1.0 - vel_edge_in[1, 2 * planes : 2 * planes + 1, :]
    columns = jnp.concatenate(
        [vel_edge_in[0, planes : 2 * planes, :], vel_edge_in[1, 0:planes, :]], axis=0
    )
    field = [
        jnp.stack([dens[pl.ds(p * cells + t, SUB, stride=mp), :] for p in range(planes)])
        for t in range(mp)
    ]
    vel_block = pos_kept = vel_kept = None

    for step in range(STEPS):
        kept = drift(step, field, row_before, row_after, columns)
        own, outer_own, first, own_end = eliminate(pos_block, kept, hold_a, hold_b)
        pos_buf[step, ipos, 0:planes, :] = first
        pos_buf[step, ipos, planes : 2 * planes, :] = own_end
        spread(*pos_args[step])
        if step == 0:
            vext[0:cells, :] = vcoef[...]
            vext[cells : cells + 1, :] = pos_edge_in[0, 2 * planes + 3 : 2 * planes + 4, :]
            vext[cells + 1 : cells + 2, :] = pos_edge_in[1, 2 * planes + 2 : 2 * planes + 3, :]
            turned[0:width, :] = vext[...].T
            vel_cbuf[ivel] = jnp.zeros((8, lanes), jnp.float32)

            def vel_row(r, value):
                vel_cbuf[ivel, r : r + 1, :] = value

            vel_block = factor_block(
                [turned[pl.ds(t, SUB, stride=mv), :] for t in range(mv)], vel_row
            )
            spread(*vel_coef_args)
            edge_each(0, lambda c, _: c.wait_send())
            edge_each(1, lambda c, _: c.wait_send())
            spread_wait_send(*pos_coef_args)
            spread_wait_recv(*pos_coef_args)
            pos_kept = reduced_coefs(pos_cbuf, npos)
        if step > 0:
            spread_wait_send(*vel_args[step - 1])
        spread_wait_recv(*pos_args[step])
        reduced_solve(pos_kept, pos_buf, step, pos_whole, npos, planes)
        before, end, beyond = pos_whole[ipos], pos_whole[ipos + 1], pos_whole[ipos + 2]
        swept = finish(pos_block, own, outer_own, before, end, hold_a, hold_b)
        for t in range(mp):
            for p in range(planes):
                ext[pl.ds(p * lanes + t, SUB, stride=mp), :] = swept[t][p]
        ext[pl.ds(cells, planes, stride=lanes), :] = before
        ext[pl.ds(cells + 1, planes, stride=lanes), :] = (
            pos_buf[step, ipos + 1, 0:planes, :]
            + pos_cbuf[ipos + 1, 0:1, :] * end
            + pos_cbuf[ipos + 1, 1:2, :] * beyond
        )
        for p in range(planes):
            turned[p * width : (p + 1) * width, :] = ext[p * lanes : (p + 1) * lanes, :].T
        source = [
            jnp.stack([turned[pl.ds(p * width + t, SUB, stride=mv), :] for p in range(planes)])
            for t in range(mv)
        ]
        own, outer_own, first, own_end = eliminate(vel_block, source, hold_a, hold_b)
        vel_buf[step, ivel, 0:planes, :] = first
        vel_buf[step, ivel, planes : 2 * planes, :] = own_end
        spread(*vel_args[step])
        spread_wait_send(*pos_args[step])
        if step == 0:
            spread_wait_send(*vel_coef_args)
            spread_wait_recv(*vel_coef_args)
            vel_kept = reduced_coefs(vel_cbuf, nvel)
        spread_wait_recv(*vel_args[step])
        reduced_solve(vel_kept, vel_buf, step, vel_whole, nvel, planes)
        before, end, beyond = vel_whole[ivel], vel_whole[ivel + 1], vel_whole[ivel + 2]
        solved = finish(vel_block, own, outer_own, before, end, hold_a, hold_b)
        for t in range(mv):
            for p in range(planes):
                turned[pl.ds(p * width + t, SUB, stride=mv), :] = solved[t][p]
        if step < STEPS - 1:
            for p in range(planes):
                ext[p * lanes : (p + 1) * lanes, :] = turned[p * width : (p + 1) * width, :].T
            field = []
            for t in range(mp):
                keep = 1.0 - mask[pl.ds(t, SUB, stride=mp), :].astype(jnp.float32)
                field.append(
                    jnp.stack(
                        [ext[pl.ds(p * lanes + t, SUB, stride=mp), :] for p in range(planes)]
                    )
                    * keep
                )
            row_before = ext[pl.ds(cells, planes, stride=lanes), :] * keep_before
            row_after = ext[pl.ds(cells + 1, planes, stride=lanes), :] * keep_after
            following = (
                vel_buf[step, ivel + 1, 0:planes, :]
                + vel_cbuf[ivel + 1, 0:1, :] * end
                + vel_cbuf[ivel + 1, 1:2, :] * beyond
            )
            columns = jnp.concatenate([before * col_keep_left, following * col_keep_right], axis=0)
        else:
            keep = 1.0 - mask[...].astype(jnp.float32)
            for p in range(planes):
                result = turned[p * width : (p + 1) * width, :].T
                out[p * cells : (p + 1) * cells, :] = result[0:cells] * keep

    spread_wait_send(*vel_args[-1])


def on_device(npos, nvel, density, pos_coef, vel_coef, exit_mask, phase_index):
    planes, cells, width = density.shape
    f32 = jnp.float32
    vmem = pl.BlockSpec(memory_space=pltpu.VMEM)
    dma = pltpu.SemaphoreType.DMA
    scratch = lambda *shape: pltpu.VMEM(shape, f32)
    field, absorbed = pl.pallas_call(
        functools.partial(kernel, npos, nvel, planes, cells, width),
        out_shape=(
            pltpu.VMEM((planes * cells, width), f32),
            pltpu.VMEM((cells, width), f32),
        ),
        in_specs=[pl.BlockSpec(memory_space=pltpu.HBM)] * 5,
        out_specs=(vmem, vmem),
        scratch_shapes=[
            scratch(planes * cells, width),
            scratch(cells, width),
            scratch(cells, width),
            pltpu.VMEM((cells, width), jnp.int32),
            pltpu.SMEM((planes,), jnp.int32),
            scratch(cells // SUB, planes, SUB, width),
            scratch(cells // SUB, planes, SUB, width),
            scratch(planes * 128, width),
            scratch(planes * width, 128),
            scratch(128, width),
            scratch(128, width),
            scratch(16, width),
            scratch(16, width),
            scratch(2, 16, width),
            scratch(2, 16, width),
            scratch(npos + 1, 8, width),
            scratch(nvel + 1, 8, width),
            scratch(STEPS, npos + 1, 2 * planes, width),
            scratch(STEPS, nvel + 1, 2 * planes, width),
            scratch(npos + 2, planes, width),
            scratch(nvel + 2, planes, width),
            scratch(planes * SUB, width),
            scratch(planes * SUB, width),
            dma((5,)),
            dma((2, 2)),
            dma((2, 2)),
            dma((1 + STEPS, npos)),
            dma((1 + STEPS, npos)),
            dma((1 + STEPS, nvel)),
            dma((1 + STEPS, nvel)),
        ],
        compiler_params=pltpu.CompilerParams(
            collective_id=0, has_side_effects=True
        ),
        cost_estimate=pl.CostEstimate(
            flops=2_000_000, bytes_accessed=400_000, transcendentals=1024
        ),
        name="line_solves",
    )(density.reshape(planes * cells, width), pos_coef, vel_coef, exit_mask, phase_index)
    return field.reshape(planes, cells, width), absorbed


def solution(mesh):
    return jax.shard_map(
        functools.partial(on_device, mesh.shape["pos"], mesh.shape["vel"]),
        mesh=mesh,
        in_specs=(P(None, "pos", "vel"), P("pos", "vel"), P("pos", "vel"), P("pos", "vel"), P()),
        out_specs=(P(None, "pos", "vel"), P("pos", "vel")),
        check_vma=False,
    )
```

```python
import functools
import math

import jax
import jax.numpy as jnp
from jax import lax
from jax.experimental import pallas as pl
from jax.experimental.pallas import tpu as pltpu
from jax.sharding import PartitionSpec as P

STEPS = 2
NPHASE = 64
SUB = 8
MESH = pl.DeviceIdType.MESH


def coef_chain(low, high, excess):
    inv, carry_low, ups, lows, rest = [], [], [], [], []
    for t in range(len(low)):
        if t == 0:
            left_low, left_rest = low[0], excess[0]
        else:
            left_low, left_rest = low[t] * lows[-1], low[t] * rest[-1] + excess[t]
        factor = 1.0 / (left_low + left_rest + high[t])
        inv.append(factor)
        carry_low.append(low[t] * factor)
        ups.append(high[t] * factor)
        lows.append(left_low * factor)
        rest.append(left_rest * factor)
    beta, gamma, eps = lows[-1], ups[-1], rest[-1]
    betas, gammas, epss = [beta], [gamma], [eps]
    for t in range(len(low) - 2, -1, -1):
        beta = lows[t] + ups[t] * beta
        gamma = ups[t] * gamma
        eps = rest[t] + ups[t] * eps
        betas.append(beta)
        gammas.append(gamma)
        epss.append(eps)
    return inv, carry_low, ups, betas[::-1], gammas[::-1], epss[::-1]


def source_chain(chain, source):
    inv, carry_low, ups = chain[:3]
    forward = [source[0] * inv[0]]
    for t in range(1, len(source)):
        forward.append(source[t] * inv[t] + carry_low[t] * forward[-1])
    own = [forward[-1]]
    for t in range(len(source) - 2, -1, -1):
        own.append(forward[t] + ups[t] * own[-1])
    return own[::-1]


def next_sub(x, axis):
    return pltpu.roll(x, SUB - 1, axis)


def factor_block(coef, store_row):
    one = jnp.ones_like(coef[0])
    inner = coef_chain(coef[:-1], coef[:-1], [one] * (len(coef) - 1))
    beta, gamma, eps = inner[3:]
    last = coef[-1]
    low = last * beta[-1]
    high = last * next_sub(gamma[0], 0)
    excess = 1.0 + last * eps[-1] + last * next_sub(eps[0], 0)
    rows = lambda x: [x[s : s + 1] for s in range(SUB - 1)]
    outer = coef_chain(rows(low), rows(high), rows(excess))
    obeta, ogamma, oeps = outer[3:]
    end = slice(SUB - 1, SUB)
    first_gamma = gamma[0][0:1]
    store_row(0, beta[0][0:1] + first_gamma * obeta[0])
    store_row(1, first_gamma * ogamma[0])
    store_row(2, eps[0][0:1] + first_gamma * oeps[0])
    store_row(3, last[end])
    store_row(4, low[end] * obeta[-1])
    store_row(5, 1.0 + last[end] * eps[-1][end] + low[end] * oeps[-1])
    return inner, outer, last, first_gamma, low[end]


def eliminate(block, source, hold_a, hold_b):
    inner, outer, last, first_gamma, end_low = block
    planes = source[0].shape[0]
    own = source_chain(inner, source[:-1])
    sub = lax.broadcasted_iota(jnp.int32, source[0].shape, 1)
    after = jnp.where(sub == SUB - 1, 0.0, next_sub(own[0], 1))
    seps = source[-1] + last * (own[-1] + after)
    hold_a[...] = seps.reshape(hold_a.shape)
    hold_b[...] = own[0].reshape(hold_b.shape)
    row = lambda ref, s: ref[pl.ds(s, planes, stride=SUB), :]
    outer_own = source_chain(outer, [row(hold_a, s) for s in range(SUB - 1)])
    first = row(hold_b, 0) + first_gamma * outer_own[0]
    own_end = row(hold_a, SUB - 1) + end_low * outer_own[-1]
    return own, outer_own, first, own_end


def finish(block, own, outer_own, before, end, hold_a, hold_b):
    inner, outer = block[:2]
    planes = before.shape[0]
    hold_b[pl.ds(0, planes, stride=SUB), :] = before
    for s in range(SUB - 1):
        value = outer_own[s] + outer[3][s] * before + outer[4][s] * end
        hold_a[pl.ds(s, planes, stride=SUB), :] = value
        hold_b[pl.ds(s + 1, planes, stride=SUB), :] = value
    hold_a[pl.ds(SUB - 1, planes, stride=SUB), :] = end
    right = hold_a[...].reshape(own[0].shape)
    left = hold_b[...].reshape(own[0].shape)
    return [p + b * left + g * right for p, b, g in zip(own, inner[3], inner[4])] + [right]


def reduced_coefs(buf, count):
    kept, rest = [], 1.0
    for d in range(count):
        link = buf[d, 3:4, :]
        left = buf[d, 4:5, :]
        high = link * buf[d + 1, 1:2, :]
        excess = left * rest + buf[d, 5:6, :] + link * buf[d + 1, 2:3, :]
        factor = 1.0 / (excess + high)
        rest = excess * factor
        kept.append((factor, left * factor, high * factor, link * factor))
    return kept


def reduced_solve(kept, buf, step, whole, count, planes):
    forward, prior = [], None
    for d in range(count):
        factor, left, _, link = kept[d]
        value = factor * buf[step, d, planes : 2 * planes, :] + link * buf[step, d + 1, 0:planes, :]
        prior = value if prior is None else value + left * prior
        forward.append(prior)
    value = forward[-1]
    whole[count] = value
    for d in range(count - 2, -1, -1):
        value = forward[d] + kept[d][2] * value
        whole[d + 1] = value


def kernel(
    npos, nvel, planes, cells, width,
    dens_in, pcoef_in, vcoef_in, mask_in, phase_in,
    out, taken,
    dens, pcoef, vcoef, mask, phase, rates_up, rates_down,
    ext, turned, edge_tmp, vext, pos_edge, vel_edge, pos_edge_in, vel_edge_in,
    pos_cbuf, vel_cbuf, pos_buf, vel_buf, pos_whole, vel_whole, hold_a, hold_b,
    load_sem, edge_send, edge_recv, psend, precv, vsend, vrecv,
):
    lanes = width
    mp, mv = cells // SUB, width // SUB
    ipos, ivel = lax.axis_index("pos"), lax.axis_index("vel")

    pos_id = lambda d: (d, ivel)
    vel_id = lambda d: (ipos, d)

    barrier = pltpu.get_barrier_semaphore()

    def greet(count, me, ident):
        for off in range(1, count):
            peer = lax.rem(me + off, count)
            pl.semaphore_signal(barrier, 1, device_id=ident(peer), device_id_type=MESH)

    loads = [
        pltpu.make_async_copy(src, dst, load_sem.at[i])
        for i, (src, dst) in enumerate(
            (
                (dens_in, dens),
                (mask_in, mask),
                (vcoef_in, vcoef),
                (pcoef_in, pcoef),
                (phase_in, phase),
            )
        )
    ]
    pos_edge_in[...] = jnp.zeros_like(pos_edge_in)
    vel_edge_in[...] = jnp.zeros_like(vel_edge_in)
    greet(npos, ipos, pos_id)
    greet(nvel, ivel, vel_id)
    for load in loads:
        load.start()
    ext[...] = jnp.zeros_like(ext)
    vext[...] = jnp.zeros_like(vext)
    edge_tmp[...] = jnp.zeros_like(edge_tmp)
    for cbuf, buf, whole, count in (
        (pos_cbuf, pos_buf, pos_whole, npos),
        (vel_cbuf, vel_buf, vel_whole, nvel),
    ):
        sub = lax.broadcasted_iota(jnp.int32, (8, lanes), 0)
        cbuf[count] = jnp.where(sub == 2, 1.0, 0.0)
        buf[0, count] = jnp.zeros((2 * planes, lanes), jnp.float32)
        buf[1, count] = jnp.zeros((2 * planes, lanes), jnp.float32)
        whole[0] = jnp.zeros((planes, lanes), jnp.float32)
        whole[count + 1] = jnp.zeros((planes, lanes), jnp.float32)

    for load in loads[:3]:
        load.wait()

    hit = mask[...].astype(jnp.float32)
    pos_edge[...] = jnp.zeros_like(pos_edge)
    for p in range(planes):
        pos_edge[p : p + 1, :] = dens[p * cells : p * cells + 1, :]
        pos_edge[planes + p : planes + p + 1, :] = dens[(p + 1) * cells - 1 : (p + 1) * cells, :]
    pos_edge[2 * planes : 2 * planes + 1, :] = hit[0:1]
    pos_edge[2 * planes + 1 : 2 * planes + 2, :] = hit[cells - 1 : cells]
    pos_edge[2 * planes + 2 : 2 * planes + 3, :] = vcoef[0:1, :]
    pos_edge[2 * planes + 3 : 2 * planes + 4, :] = vcoef[cells - 1 : cells, :]
    lane = lax.broadcasted_iota(jnp.int32, (cells, lanes), 1)
    gathered = jnp.zeros((cells, lanes), jnp.float32)
    for p in range(planes):
        one = dens[p * cells : (p + 1) * cells, :]
        gathered = jnp.where(lane == p, one[:, 0:1], gathered)
        gathered = jnp.where(lane == planes + p, one[:, lanes - 1 : lanes], gathered)
    gathered = jnp.where(lane == 2 * planes, hit[:, 0:1], gathered)
    gathered = jnp.where(lane == 2 * planes + 1, hit[:, lanes - 1 : lanes], gathered)
    edge_tmp[0:cells, :] = gathered
    vel_edge[...] = edge_tmp[...].T[0:16]

    def edge_copy(axis, to_right, src, dst, ident, me):
        slot = 0 if to_right else 1
        peer = me + 1 if to_right else me - 1
        return pltpu.make_async_remote_copy(
            src_ref=src, dst_ref=dst.at[slot],
            send_sem=edge_send.at[axis, slot], recv_sem=edge_recv.at[axis, slot],
            device_id=ident(peer), device_id_type=MESH,
        )

    sides = (
        (0, pos_edge, pos_edge_in, pos_id, ipos, npos),
        (1, vel_edge, vel_edge_in, vel_id, ivel, nvel),
    )

    def edge_each(which, act):
        axis, src, dst, ident, me, count = sides[which]

        @pl.when(me < count - 1)
        def _():
            act(edge_copy(axis, True, src, dst, ident, me), True)

        @pl.when(me > 0)
        def _():
            act(edge_copy(axis, False, src, dst, ident, me), False)

    def edge_wait(which):
        axis, src, dst, ident, me, count = sides[which]

        @pl.when(me > 0)
        def _():
            edge_copy(axis, True, src, dst, ident, me).wait_recv()

        @pl.when(me < count - 1)
        def _():
            edge_copy(axis, False, src, dst, ident, me).wait_recv()

    def spread_copy(ref, kind, sends, recvs, ident, me, count, off):
        peer = lax.rem(me + off, count)
        return pltpu.make_async_remote_copy(
            src_ref=ref.at[me], dst_ref=ref.at[me],
            send_sem=sends.at[kind, off], recv_sem=recvs.at[kind, me],
            device_id=ident(peer), device_id_type=MESH,
        )

    def spread(*args):
        for off in range(1, args[-1]):
            spread_copy(*args, off).start()

    def spread_wait_recv(ref, kind, sends, recvs, ident, me, count):
        for off in range(1, count):
            sender = lax.rem(me + off, count)
            pltpu.make_async_remote_copy(
                src_ref=ref.at[sender], dst_ref=ref.at[sender],
                send_sem=sends.at[kind, off], recv_sem=recvs.at[kind, sender],
                device_id=ident(sender), device_id_type=MESH,
            ).wait_recv()

    def spread_wait_send(*args):
        for off in range(1, args[-1]):
            spread_copy(*args, off).wait_send()

    pos_coef_args = (pos_cbuf, 0, psend, precv, pos_id, ipos, npos)
    vel_coef_args = (vel_cbuf, 0, vsend, vrecv, vel_id, ivel, nvel)
    pos_args = [(pos_buf.at[i], 1 + i, psend, precv, pos_id, ipos, npos) for i in range(STEPS)]
    vel_args = [(vel_buf.at[i], 1 + i, vsend, vrecv, vel_id, ivel, nvel) for i in range(STEPS)]

    pl.semaphore_wait(barrier, (npos - 1) + (nvel - 1))
    edge_each(0, lambda c, _: c.start())
    edge_each(1, lambda c, _: c.start())

    for load in loads[3:]:
        load.wait()
    pos_cbuf[ipos] = jnp.zeros((8, lanes), jnp.float32)

    def pos_row(r, value):
        pos_cbuf[ipos, r : r + 1, :] = value

    pos_block = factor_block([pcoef[pl.ds(t, SUB, stride=mp), :] for t in range(mp)], pos_row)
    spread(*pos_coef_args)

    sub = lax.broadcasted_iota(jnp.int32, (SUB, lanes), 0)
    lane = lax.broadcasted_iota(jnp.int32, (SUB, lanes), 1)
    turns = jnp.zeros((SUB, lanes), jnp.int32)
    for p in range(planes):
        turns = jnp.where(sub == p, phase[p], turns)
    cosine = 0.6 * jnp.cos(2.0 * math.pi * turns.astype(jnp.float32) / NPHASE)
    vpos = (2.0 * (ivel * width + lane).astype(jnp.float32) + 1.0) * (1.0 / (width * nvel)) - 1.0
    move = 0.45 * vpos
    move_up, move_down = jnp.maximum(move, 0.0), jnp.minimum(move, 0.0)
    cosines = jnp.stack([jnp.broadcast_to(cosine[p : p + 1], (SUB, lanes)) for p in range(planes)])

    for t in range(mp):
        xpos = 1.5 * (
            (2.0 * (ipos * cells + sub * mp + t).astype(jnp.float32) + 1.0) * (1.0 / (cells * npos))
            - 1.0
        )
        rate = 0.15 * (((xpos - xpos * xpos * xpos)[None] + cosines) - (0.5 * vpos)[None])
        rates_up[t] = jnp.maximum(rate, 0.0)
        rates_down[t] = jnp.minimum(rate, 0.0)

    def drift(step, field, row_before, row_after, columns):
        edge_tmp[0 : 2 * planes, :] = columns
        if step > 0:
            edge_tmp[2 * planes : 16, :] = jnp.zeros((16 - 2 * planes, lanes), jnp.float32)
        turned[0:lanes, :] = edge_tmp[...].T
        wide_sub = lax.broadcasted_iota(jnp.int32, (planes, SUB, lanes), 1)
        wide_lane = lax.broadcasted_iota(jnp.int32, (planes, SUB, lanes), 2)
        before = jnp.where(wide_sub == 0, row_before[:, None, :], pltpu.roll(field[-1], 1, 1))
        after = jnp.where(wide_sub == SUB - 1, row_after[:, None, :], next_sub(field[0], 1))
        kept = []
        for t in range(mp):
            center = field[t]
            back = field[t - 1] if t else before
            ahead = field[t + 1] if t < mp - 1 else after
            cols = turned[pl.ds(t, SUB, stride=mp), :]
            left = jnp.stack([cols[:, p : p + 1] for p in range(planes)])
            right = jnp.stack([cols[:, planes + p : planes + p + 1] for p in range(planes)])
            back_v = jnp.where(wide_lane == 0, left, pltpu.roll(center, 1, 2))
            ahead_v = jnp.where(wide_lane == lanes - 1, right, pltpu.roll(center, lanes - 1, 2))
            along_x = move_up * (center - back) + move_down * (ahead - center)
            along_v = rates_up[t] * (center - back_v) + rates_down[t] * (ahead_v - center)
            drifted = center - along_x - along_v
            hit_t = mask[pl.ds(t, SUB, stride=mp), :].astype(jnp.float32)
            took = jnp.sum(drifted, axis=0) * hit_t
            if step > 0:
                took = taken[pl.ds(t, SUB, stride=mp), :] + took
            taken[pl.ds(t, SUB, stride=mp), :] = took
            kept.append(drifted * (1.0 - hit_t))
        return kept

    edge_wait(1)
    edge_wait(0)
    row_before = pos_edge_in[0, planes : 2 * planes, :]
    row_after = pos_edge_in[1, 0:planes, :]
    keep_before = 1.0 - pos_edge_in[0, 2 * planes + 1 : 2 * planes + 2, :]
    keep_after = 1.0 - pos_edge_in[1, 2 * planes : 2 * planes + 1, :]
    col_keep_left = 1.0 - vel_edge_in[0, 2 * planes + 1 : 2 * planes + 2, :]
    col_keep_right = 1.0 - vel_edge_in[1, 2 * planes : 2 * planes + 1, :]
    columns = jnp.concatenate(
        [vel_edge_in[0, planes : 2 * planes, :], vel_edge_in[1, 0:planes, :]], axis=0
    )
    field = [
        jnp.stack([dens[pl.ds(p * cells + t, SUB, stride=mp), :] for p in range(planes)])
        for t in range(mp)
    ]
    vel_block = pos_kept = vel_kept = None

    for step in range(STEPS):
        kept = drift(step, field, row_before, row_after, columns)
        own, outer_own, first, own_end = eliminate(pos_block, kept, hold_a, hold_b)
        pos_buf[step, ipos, 0:planes, :] = first
        pos_buf[step, ipos, planes : 2 * planes, :] = own_end
        spread(*pos_args[step])
        if step == 0:
            vext[0:cells, :] = vcoef[...]
            vext[cells : cells + 1, :] = pos_edge_in[0, 2 * planes + 3 : 2 * planes + 4, :]
            vext[cells + 1 : cells + 2, :] = pos_edge_in[1, 2 * planes + 2 : 2 * planes + 3, :]
            turned[0:width, :] = vext[...].T
            vel_cbuf[ivel] = jnp.zeros((8, lanes), jnp.float32)

            def vel_row(r, value):
                vel_cbuf[ivel, r : r + 1, :] = value

            vel_block = factor_block(
                [turned[pl.ds(t, SUB, stride=mv), :] for t in range(mv)], vel_row
            )
            spread(*vel_coef_args)
            edge_each(0, lambda c, _: c.wait_send())
            edge_each(1, lambda c, _: c.wait_send())
            spread_wait_send(*pos_coef_args)
            spread_wait_recv(*pos_coef_args)
            pos_kept = reduced_coefs(pos_cbuf, npos)
        if step > 0:
            spread_wait_send(*vel_args[step - 1])
        spread_wait_recv(*pos_args[step])
        reduced_solve(pos_kept, pos_buf, step, pos_whole, npos, planes)
        before, end, beyond = pos_whole[ipos], pos_whole[ipos + 1], pos_whole[ipos + 2]
        swept = finish(pos_block, own, outer_own, before, end, hold_a, hold_b)
        for t in range(mp):
            for p in range(planes):
                ext[pl.ds(p * lanes + t, SUB, stride=mp), :] = swept[t][p]
        if step < STEPS - 1:
            ext[pl.ds(cells, planes, stride=lanes), :] = before
            ext[pl.ds(cells + 1, planes, stride=lanes), :] = (
                pos_buf[step, ipos + 1, 0:planes, :]
                + pos_cbuf[ipos + 1, 0:1, :] * end
                + pos_cbuf[ipos + 1, 1:2, :] * beyond
            )
        for p in range(planes):
            turned[p * width : (p + 1) * width, :] = ext[p * lanes : (p + 1) * lanes, :].T
        source = [
            jnp.stack([turned[pl.ds(p * width + t, SUB, stride=mv), :] for p in range(planes)])
            for t in range(mv)
        ]
        own, outer_own, first, own_end = eliminate(vel_block, source, hold_a, hold_b)
        vel_buf[step, ivel, 0:planes, :] = first
        vel_buf[step, ivel, planes : 2 * planes, :] = own_end
        spread(*vel_args[step])
        spread_wait_send(*pos_args[step])
        if step == 0:
            spread_wait_send(*vel_coef_args)
            spread_wait_recv(*vel_coef_args)
            vel_kept = reduced_coefs(vel_cbuf, nvel)
        spread_wait_recv(*vel_args[step])
        reduced_solve(vel_kept, vel_buf, step, vel_whole, nvel, planes)
        before, end, beyond = vel_whole[ivel], vel_whole[ivel + 1], vel_whole[ivel + 2]
        solved = finish(vel_block, own, outer_own, before, end, hold_a, hold_b)
        for t in range(mv):
            for p in range(planes):
                turned[pl.ds(p * width + t, SUB, stride=mv), :] = solved[t][p]
        if step < STEPS - 1:
            for p in range(planes):
                ext[p * lanes : (p + 1) * lanes, :] = turned[p * width : (p + 1) * width, :].T
            field = []
            for t in range(mp):
                keep = 1.0 - mask[pl.ds(t, SUB, stride=mp), :].astype(jnp.float32)
                field.append(
                    jnp.stack(
                        [ext[pl.ds(p * lanes + t, SUB, stride=mp), :] for p in range(planes)]
                    )
                    * keep
                )
            row_before = ext[pl.ds(cells, planes, stride=lanes), :] * keep_before
            row_after = ext[pl.ds(cells + 1, planes, stride=lanes), :] * keep_after
            following = (
                vel_buf[step, ivel + 1, 0:planes, :]
                + vel_cbuf[ivel + 1, 0:1, :] * end
                + vel_cbuf[ivel + 1, 1:2, :] * beyond
            )
            columns = jnp.concatenate([before * col_keep_left, following * col_keep_right], axis=0)
        else:
            keep = 1.0 - mask[...].astype(jnp.float32)
            for p in range(planes):
                result = turned[p * width : (p + 1) * width, :].T
                out[p * cells : (p + 1) * cells, :] = result[0:cells] * keep

    spread_wait_send(*vel_args[-1])


def on_device(npos, nvel, density, pos_coef, vel_coef, exit_mask, phase_index):
    planes, cells, width = density.shape
    f32 = jnp.float32
    vmem = pl.BlockSpec(memory_space=pltpu.VMEM)
    dma = pltpu.SemaphoreType.DMA
    scratch = lambda *shape: pltpu.VMEM(shape, f32)
    field, absorbed = pl.pallas_call(
        functools.partial(kernel, npos, nvel, planes, cells, width),
        out_shape=(
            pltpu.VMEM((planes * cells, width), f32),
            pltpu.VMEM((cells, width), f32),
        ),
        in_specs=[pl.BlockSpec(memory_space=pltpu.HBM)] * 5,
        out_specs=(vmem, vmem),
        scratch_shapes=[
            scratch(planes * cells, width),
            scratch(cells, width),
            scratch(cells, width),
            pltpu.VMEM((cells, width), jnp.int32),
            pltpu.SMEM((planes,), jnp.int32),
            scratch(cells // SUB, planes, SUB, width),
            scratch(cells // SUB, planes, SUB, width),
            scratch(planes * 128, width),
            scratch(planes * width, 128),
            scratch(128, width),
            scratch(128, width),
            scratch(16, width),
            scratch(16, width),
            scratch(2, 16, width),
            scratch(2, 16, width),
            scratch(npos + 1, 8, width),
            scratch(nvel + 1, 8, width),
            scratch(STEPS, npos + 1, 2 * planes, width),
            scratch(STEPS, nvel + 1, 2 * planes, width),
            scratch(npos + 2, planes, width),
            scratch(nvel + 2, planes, width),
            scratch(planes * SUB, width),
            scratch(planes * SUB, width),
            dma((5,)),
            dma((2, 2)),
            dma((2, 2)),
            dma((1 + STEPS, npos)),
            dma((1 + STEPS, npos)),
            dma((1 + STEPS, nvel)),
            dma((1 + STEPS, nvel)),
        ],
        compiler_params=pltpu.CompilerParams(
            collective_id=0, has_side_effects=True
        ),
        cost_estimate=pl.CostEstimate(
            flops=2_000_000, bytes_accessed=400_000, transcendentals=1024
        ),
        name="line_solves",
    )(density.reshape(planes * cells, width), pos_coef, vel_coef, exit_mask, phase_index)
    return field.reshape(planes, cells, width), absorbed


def solution(mesh):
    return jax.shard_map(
        functools.partial(on_device, mesh.shape["pos"], mesh.shape["vel"]),
        mesh=mesh,
        in_specs=(P(None, "pos", "vel"), P("pos", "vel"), P("pos", "vel"), P("pos", "vel"), P()),
        out_specs=(P(None, "pos", "vel"), P("pos", "vel")),
        check_vma=False,
    )
```
